256 devices in a mesh: lon: 16 (over y_lo, z), lat: 16 (over x, y_hi, core).
Axes of the slice: x: 4, y: 4 (y_hi: 2, y_lo: 2; y = y_hi * 2 + y_lo), z: 8, core: 2. Of those that a mesh axis runs over, the one named last changes fastest.
Arguments:
- tracers: float32 [4, 8, 256, 2048], P(None, None, 'lat', 'lon'), may hold values from -6 to 6
- courant_frac: float32 [8, 256, 2048], P(None, 'lat', 'lon'), may hold values from 0 to 1
- shifts: int32 [8, 256], P(None, 'lat'), may hold values from -384 to 383
- merid: float32 [8, 256, 2048], P(None, 'lat', 'lon'), may hold values from -0.9 to 0.9
Outputs:
- updated: float32 [4, 8, 256, 2048], P(None, None, 'lat', 'lon')
- zonal_flux: float32 [4, 8, 256, 2048], P(None, None, 'lat', 'lon')
The draws below stay inside these ranges and needn't reach their ends.
All inputs are finite; a program needn't handle non-finite values.
Results may differ from the reference program's by a relative error of at most 0.0003.
Values sent between devices are 32-bit elements; how exact they have to be, the bound alone decides.
A program may use at most 64 MiB of HBM per device.

```python
import jax
import jax.numpy as jnp
from jax import lax

TRACERS = 4
LEV = 8
LON_DEV = 128
REACH = 3
NLAT = 256
NLON = 2048


def draw_shifts(key, part):
    rows = jnp.arange(NLAT, dtype=jnp.int32)
    spread = jnp.abs(2 * rows + 1 - NLAT)
    top = REACH * LON_DEV
    reach_row = 1 + (top - 1) * (spread * spread // (NLAT - 1)) // (NLAT - 1)
    reach_row = reach_row[None, :]
    raw_key = jax.random.fold_in(key, 11)
    sign_key = jax.random.fold_in(key, 23)
    raw = jax.random.randint(raw_key, (LEV, NLAT), 0, 1 << 20, dtype=jnp.int32)
    values = raw % (2 * reach_row) - reach_row
    signs = jax.random.randint(sign_key, (LEV, NLAT), 0, 2, dtype=jnp.int32)
    polar = (spread == NLAT - 1)[None, :]
    values = jnp.where(polar, jnp.where(signs == 1, -reach_row, reach_row - 1), values)
    level_ids = jnp.arange(LEV, dtype=jnp.int32)[:, None]
    row_ids = rows[None, :]
    values = jnp.where((level_ids == 0) & (row_ids == 0), -top, values)
    values = jnp.where((level_ids == 0) & (row_ids == NLAT - 1), top - 1, values)
    return values.astype(jnp.int32)


def block_levels(rng, extent, pieces, low, high):
    def one(axis_at, shards_of):
        draws = jax.random.uniform(jax.random.fold_in(jax.random.fold_in(rng, 6), axis_at), (shards_of,), jnp.float32, low / len(pieces), high / len(pieces))
        return jnp.repeat(jnp.exp(draws), extent[axis_at] // shards_of).reshape((-1,) + (1,) * (len(extent) - axis_at - 1))

    level = one(*pieces[0])
    for cut in pieces[1:]:
        level = level * one(*cut)
    return level


def bell_draw(own_key, shape, scale, bound, cuts=(), held_as=jnp.bfloat16):
    level = block_levels(own_key, shape, cuts, -0.22, 0.18) if cuts else 1.0
    values = jax.random.normal(own_key, shape, jnp.float32) * scale * level
    return jnp.minimum(jnp.maximum(values, -bound), bound).astype(held_as)


def setup_inputs(seed: int = 0) -> dict:
    streams_of = jax.random.split(jax.random.key(seed), 5)
    return {
        "tracers": bell_draw(streams_of[0], (TRACERS, LEV, NLAT, NLON), 1.0, 6.0, ((2, 16), (3, 16)), jnp.float32),
        "courant_frac": jnp.clip(1.0 * jax.random.uniform(streams_of[1], (LEV, NLAT, NLON), jnp.float32) ** block_levels(streams_of[1], (LEV, NLAT, NLON), ((1, 16), (2, 16)), -0.2, 0.2), 0.0, 1.0),
        "shifts": draw_shifts(jax.random.fold_in(streams_of[4], 71), 0),
        "merid": jnp.clip(jax.random.uniform(streams_of[3], (LEV, NLAT, NLON), jnp.float32, -0.9, 0.9) * block_levels(streams_of[3], (LEV, NLAT, NLON), ((1, 16), (2, 16)), -0.4, 0.0), -0.9, 0.9),
    }


def cell_part(values, slopes, weight):
    return values * weight + slopes * (weight * weight - weight) * 0.5


def advance(field, courant_frac, shifts, merid):
    levels, nrows, nlons = field.shape
    nblock = nlons // LON_DEV
    slopes = 0.5 * (jnp.roll(field, -1, axis=2) - jnp.roll(field, 1, axis=2))
    field_blocks = field.reshape(levels, nrows, nblock, LON_DEV)
    slope_blocks = slopes.reshape(levels, nrows, nblock, LON_DEV)
    totals = jnp.sum(field_blocks, axis=3)
    start_cell = (-1 - shifts).astype(jnp.int32)
    low_block = jnp.floor_divide(start_cell, LON_DEV).astype(jnp.int32)
    remain = (start_cell - low_block * LON_DEV).astype(jnp.int32)
    block_ids = jnp.arange(nblock, dtype=jnp.int32)[None, None, :]
    low_ids = (block_ids + low_block[:, :, None]) % nblock
    high_ids = (low_ids + 1) % nblock
    full_low = jnp.broadcast_to(low_ids[..., None], field_blocks.shape).astype(jnp.int32)
    full_high = jnp.broadcast_to(high_ids[..., None], field_blocks.shape).astype(jnp.int32)
    low_q = jnp.take_along_axis(field_blocks, full_low, axis=2)
    high_q = jnp.take_along_axis(field_blocks, full_high, axis=2)
    low_s = jnp.take_along_axis(slope_blocks, full_low, axis=2)
    high_s = jnp.take_along_axis(slope_blocks, full_high, axis=2)
    selector = low_block[:, :, None]
    offset_sum = jnp.zeros_like(totals)
    running = jnp.zeros_like(totals)
    for distance in range(1, REACH + 1):
        running = running + jnp.roll(totals, distance, axis=2)
        offset_sum = jnp.where(selector == -distance, -running, offset_sum)
    running = jnp.zeros_like(totals)
    for distance in range(REACH - 1):
        running = running + jnp.roll(totals, -distance, axis=2)
        offset_sum = jnp.where(selector == distance + 1, running, offset_sum)
    window_q = jnp.concatenate((low_q, high_q), axis=3)
    window_s = jnp.concatenate((low_s, high_s), axis=3)
    window_pre = jnp.cumsum(window_q, axis=3) - window_q
    cell_index = jnp.arange(LON_DEV, dtype=jnp.int32)
    index_west = jnp.broadcast_to(remain[:, :, None, None] + cell_index, field_blocks.shape).astype(jnp.int32)
    index_east = index_west + 1
    own_incl = jnp.cumsum(field_blocks, axis=3)
    own_excl = own_incl - field_blocks
    weight_east = (1.0 - courant_frac).reshape(levels, nrows, nblock, LON_DEV)
    weight_west = (1.0 - jnp.roll(courant_frac, 1, axis=2)).reshape(levels, nrows, nblock, LON_DEV)

    def pick(source, index):
        return jnp.take_along_axis(source, index, axis=3)

    flux_east = own_incl - (offset_sum[..., None] + pick(window_pre, index_east)) - cell_part(pick(window_q, index_east), pick(window_s, index_east), weight_east)
    flux_west = own_excl - (offset_sum[..., None] + pick(window_pre, index_west)) - cell_part(pick(window_q, index_west), pick(window_s, index_west), weight_west)
    flux_east = flux_east.reshape(levels, nrows, nlons)
    flux_west = flux_west.reshape(levels, nrows, nlons)
    row_ids = jnp.arange(nrows, dtype=jnp.int32)[None, :, None]
    padded = jnp.pad(field, ((0, 0), (1, 1), (0, 0)))
    side_y = 0.5 * (padded[:, 2:] - padded[:, :-2])
    side_y = jnp.where((row_ids == 0) | (row_ids == nrows - 1), 0.0, side_y)
    north_v = jnp.where(row_ids == nrows - 1, 0.0, merid)
    zero_row = jnp.zeros_like(field[:, :1])
    upper_q = jnp.concatenate((field[:, 1:], zero_row), axis=1)
    upper_s = jnp.concatenate((side_y[:, 1:], zero_row), axis=1)
    north_flux = jnp.where(north_v >= 0.0, north_v * field + north_v * (1.0 - north_v) * 0.5 * side_y, north_v * upper_q - north_v * (1.0 + north_v) * 0.5 * upper_s)
    south_flux = jnp.concatenate((zero_row, north_flux[:, :-1]), axis=1)
    updated = field - (flux_east - flux_west) - (north_flux - south_flux)
    return updated, flux_east


def reference(tracers, courant_frac, shifts, merid):
    def one_tracer(field):
        return advance(field, courant_frac, shifts, merid)

    updated, zonal_flux = lax.map(one_tracer, tracers)
    return updated, zonal_flux
```

```python
import functools

import jax
import jax.numpy as jnp
from jax import lax
from jax.experimental import pallas as pl
from jax.experimental.pallas import tpu as pltpu
from jax.sharding import PartitionSpec as P

TR, LEV, ROWS, LON, RING, BANDS = 4, 8, 16, 128, 16, 16
HALF = 8
REACH = 3
MESH = pl.DeviceIdType.MESH
ORDER = tuple(z + 8 * y for z in range(8) for y in range(2))


def lanes_iota(rows):
    return lax.broadcasted_iota(jnp.int32, (rows, LON), 1)


def rows_iota(rows):
    return lax.broadcasted_iota(jnp.int32, (rows, LON), 0)


def take(values, index):
    return jnp.take_along_axis(values, index, axis=1, mode="promise_in_bounds")


def kernel(
    q_hbm, c_hbm, s_ref, v_hbm, upd_ref, flux_ref,
    qx, mx, cv, gat, ret, back, pack, base, cw_out, cw_in,
    s1, r1, s2, r2, sl, sh, rh, se, re,
):
    me = lax.axis_index("lon")
    lat = lax.axis_index("lat")
    east, west = lax.rem(me + 1, RING), lax.rem(me + RING - 1, RING)
    north, south = lax.rem(lat + 1, BANDS), lax.rem(lat + BANDS - 1, BANDS)

    barrier = pltpu.get_barrier_semaphore()
    for d in range(1, RING):
        pl.semaphore_signal(barrier, inc=1, device_id={"lon": lax.rem(me + d, RING)}, device_id_type=MESH)
    for peer in (north, south):
        pl.semaphore_signal(barrier, inc=1, device_id={"lat": peer}, device_id_type=MESH)

    def of_home(h):
        return q_hbm.at[:, h // 2, pl.ds(pl.multiple_of((h % 2) * HALF, HALF), HALF), :]

    own = pltpu.make_async_copy(of_home(me), gat.at[me], sl.at[0])
    own_q = pltpu.make_async_copy(q_hbm, qx.at[:, :, pl.ds(8, ROWS), :], sl.at[1])
    own_v = pltpu.make_async_copy(v_hbm, mx.at[:, pl.ds(8, ROWS), :], sl.at[2])
    own_c = pltpu.make_async_copy(c_hbm, cv, sl.at[3])
    own_c.start()
    own.start()
    own_q.start()
    own_v.start()
    pl.semaphore_wait(barrier, RING + 1)

    def gather_copy(d):
        target = lax.rem(me + d, RING)
        return pltpu.make_async_remote_copy(
            of_home(target), gat.at[me], s1.at[d], r1.at[d], device_id={"lon": target}, device_id_type=MESH
        )

    for d in range(1, RING):
        gather_copy(d).start()

    halo = [
        (q_hbm.at[:, :, pl.ds(ROWS - 2, 2), :], qx.at[:, :, pl.ds(6, 2), :], north),
        (q_hbm.at[:, :, pl.ds(0, 2), :], qx.at[:, :, pl.ds(24, 2), :], south),
        (v_hbm.at[:, pl.ds(ROWS - 1, 1), :], mx.at[:, pl.ds(7, 1), :], north),
    ]
    halo = [
        pltpu.make_async_remote_copy(a, b, sh.at[i], rh.at[i], device_id={"lat": p}, device_id_type=MESH)
        for i, (a, b, p) in enumerate(halo)
    ]
    for copy in halo:
        copy.start()

    lane8, row8 = lanes_iota(HALF), rows_iota(HALF)
    own_c.wait()
    packed = jnp.zeros((HALF, LON), jnp.float32)
    for tile in range(2 * LEV):
        column = cv[tile // 2, HALF * (tile % 2) : HALF * (tile % 2) + HALF, LON - 1 : LON]
        packed = jnp.where(lane8 == HALF * tile + row8, column, packed)
    cw_out[...] = jnp.broadcast_to(jnp.sum(packed, axis=0, keepdims=True), (HALF, LON))
    edge = pltpu.make_async_remote_copy(
        cw_out, cw_in, se.at[0], re.at[0], device_id={"lon": east}, device_id_type=MESH
    )
    edge.start()

    lev = me // 2
    line = s_ref[pl.ds(lev, 1), :].astype(jnp.float32)
    pick = lax.broadcasted_iota(jnp.int32, (HALF, ROWS), 1) == (
        lax.broadcasted_iota(jnp.int32, (HALF, ROWS), 0) + HALF * (me % 2)
    )
    shift = jnp.sum(jnp.where(pick, jnp.broadcast_to(line, (HALF, ROWS)), 0.0), axis=1, keepdims=True)
    first = -1 - jnp.broadcast_to(shift, (HALF, LON)).astype(jnp.int32)
    raised = first + REACH * LON
    low = jnp.right_shift(raised, 7)
    remain = jnp.bitwise_and(raised, LON - 1)
    hop = jnp.where(lane8 >= remain, low, low + 1)
    bits = [jnp.bitwise_and(hop, 1 << n) != 0 for n in range(3)]
    turn = jnp.bitwise_and(lane8 + remain, LON - 1)
    signs = []
    for off in range(-REACH, REACH):
        cell = off * LON + lane8
        if off < 0:
            signs.append(jnp.where(cell >= first, -1.0, 0.0))
        else:
            signs.append(jnp.where(cell < first, 1.0, 0.0))
    group = lane8 // (TR * HALF)
    ends = jnp.where(group == 0, LON - 1, jnp.where(group == 1, 0, 1))

    own.wait()
    for d in range(1, RING):
        gather_copy(d).wait_recv()

    def home(tr, carry):
        blocks = [gat[b, tr] for b in range(RING)]
        mine = (lane8 // HALF) % TR == tr
        mine = mine & (lane8 % HALF == row8)
        one = [jnp.where(bits[0], blocks[(b - 2) % RING], blocks[(b - 3) % RING]) for b in range(RING)]
        two = [jnp.where(bits[1], one[(b + 2) % RING], one[b]) for b in range(RING)]
        aligned = [take(jnp.where(bits[2], two[(b + 4) % RING], two[b]), turn) for b in range(RING)]
        tips = [take(a, ends) for a in aligned]
        rows = pl.ds(pl.multiple_of(tr * HALF, HALF), HALF)
        for b in range(RING):
            ret[b, rows, :] = aligned[b]
            total = blocks[(b - REACH) % RING] * signs[0]
            for n in range(1, 2 * REACH):
                total = total + blocks[(b - REACH + n) % RING] * signs[n]
            offset = jnp.sum(total, axis=1, keepdims=True)
            extra = jnp.where(group == 0, tips[b - 1], jnp.where(group == 3, offset, tips[(b + 1) % RING]))
            pack[b] = jnp.where(mine, extra, pack[b])
        return carry

    for b in range(RING):
        pack[b] = jnp.zeros((HALF, LON), jnp.float32)
    lax.fori_loop(0, TR, home, 0)
    for b in range(RING):
        ret[b, TR * HALF : TR * HALF + 1, :] = jnp.sum(pack[b], axis=0, keepdims=True)

    size = TR * HALF + 1

    def return_copy(t):
        return pltpu.make_async_remote_copy(
            ret.at[t, pl.ds(0, size)], back.at[me, pl.ds(0, size)], s2.at[t], r2.at[me],
            device_id={"lon": t}, device_id_type=MESH,
        )

    for t in ORDER:
        @pl.when(t != me)
        def _():
            return_copy(t).start()

    own_back = pltpu.make_async_copy(ret.at[me, pl.ds(0, size)], back.at[me, pl.ds(0, size)], r2.at[me])
    own_back.start()

    own_q.wait()
    own_v.wait()
    for copy in halo:
        copy.wait_recv()
    face = lat * ROWS + rows_iota(ROWS)

    def meridional(l, carry):
        for o in (-1, 0):
            v = mx[l, 8 + o : 24 + o]
            v = jnp.where((face + o == NLAT - 1) | (face + o < 0), 0.0, v)
            up = v >= 0.0
            half_low = v * (1.0 - v) * 0.5
            half_high = v * (1.0 + v) * 0.5
            zero_low = (face + o <= 0) | (face + o >= NLAT - 1)
            zero_high = (face + o + 1 <= 0) | (face + o + 1 >= NLAT - 1)
            for tr in range(TR):
                q_low = qx[tr, l, 8 + o : 24 + o]
                q_high = qx[tr, l, 9 + o : 25 + o]
                side_low = jnp.where(zero_low, 0.0, 0.5 * (q_high - qx[tr, l, 7 + o : 23 + o]))
                side_high = jnp.where(zero_high, 0.0, 0.5 * (qx[tr, l, 10 + o : 26 + o] - q_low))
                flux = jnp.where(up, v * q_low + half_low * side_low, v * q_high - half_high * side_high)
                if o < 0:
                    base[tr, l] = qx[tr, l, 8:24] + flux
                else:
                    base[tr, l] = base[tr, l] - flux
        return carry

    lax.fori_loop(0, LEV, meridional, 0)

    edge.wait_recv()
    west_row = jnp.broadcast_to(cw_in[0:1, :], (HALF, LON))
    upper = jnp.where(
        lax.broadcasted_iota(jnp.int32, (LON, LON), 0) <= lax.broadcasted_iota(jnp.int32, (LON, LON), 1), 1.0, 0.0
    ).astype(jnp.bfloat16)
    lane32, row32 = lanes_iota(TR * HALF), rows_iota(TR * HALF)
    index_a = jnp.where(lane32 == LON - 2, 1, jnp.where(lane32 == LON - 1, 2, 0)) * (TR * HALF) + row32
    index_b = jnp.where(lane32 == LON - 1, 1, 3) * (TR * HALF) + row32

    def finish(h, carry):
        pltpu.make_async_copy(ret.at[h, pl.ds(0, size)], back.at[h, pl.ds(0, size)], r2.at[h]).wait()
        l = h // 2
        start = pl.multiple_of((h % 2) * HALF, HALF)
        cells = back[h, 0 : TR * HALF]
        extra = jnp.broadcast_to(back[h, TR * HALF : TR * HALF + 1], (TR * HALF, LON))
        ext_a, ext_b = take(extra, index_a), take(extra, index_b)
        plus1 = jnp.where(lane32 == LON - 1, ext_b, pltpu.roll(cells, LON - 1, 1))
        plus2 = jnp.where(lane32 >= LON - 2, ext_a, pltpu.roll(cells, LON - 2, 1))
        q = jnp.concatenate([qx[tr, l, pl.ds(start + 8, HALF), :] for tr in range(TR)], axis=0)
        diff = q - cells
        part0 = diff.astype(jnp.bfloat16)
        rest = diff - part0.astype(jnp.float32)
        part1 = rest.astype(jnp.bfloat16)
        part2 = (rest - part1.astype(jnp.float32)).astype(jnp.bfloat16)
        sums = (
            jnp.dot(part2, upper, preferred_element_type=jnp.float32)
            + jnp.dot(part1, upper, preferred_element_type=jnp.float32)
        ) + jnp.dot(part0, upper, preferred_element_type=jnp.float32)
        c = cv[l, pl.ds(start, HALF), :]
        t = 1.0 - c
        tt = (t * t - t) * 0.25
        t_west = 1.0 - take(west_row, HALF * h + row8)
        tt_west = (t_west * t_west - t_west) * 0.25
        t, tt, t_west, tt_west = (jnp.concatenate([x] * TR, axis=0) for x in (t, tt, t_west, tt_west))
        offset = jnp.broadcast_to(ext_b[:, 0:1], (TR * HALF, LON))
        flux = sums - offset - (plus1 * t + (plus2 - cells) * tt)
        first_west = -ext_b - (cells * t_west + (plus1 - ext_a) * tt_west)
        flux_west = jnp.where(lane32 == 0, first_west, pltpu.roll(flux, 1, 1))
        change = flux - flux_west
        for tr in range(TR):
            rows = slice(tr * HALF, (tr + 1) * HALF)
            flux_ref[tr, l, pl.ds(start, HALF), :] = flux[rows]
            upd_ref[tr, l, pl.ds(start, HALF), :] = base[tr, l, pl.ds(start, HALF), :] - change[rows]
        return carry

    lax.fori_loop(0, RING, finish, 0)

    for d in range(1, RING):
        gather_copy(d).wait_send()
    for copy in halo:
        copy.wait_send()
    edge.wait_send()
    for t in ORDER:
        @pl.when(t != me)
        def _():
            return_copy(t).wait_send()


NLAT = ROWS * BANDS


def per_device(tracers, courant_frac, shifts, merid):
    vmem, dma, f32 = pltpu.VMEM, pltpu.SemaphoreType.DMA, jnp.float32
    shape = jax.ShapeDtypeStruct((TR, LEV, ROWS, LON), f32)
    anywhere, inside = pl.BlockSpec(memory_space=pl.ANY), pl.BlockSpec(memory_space=pltpu.VMEM)
    return pl.pallas_call(
        kernel,
        out_shape=(shape, shape),
        in_specs=[anywhere, anywhere, inside, anywhere],
        out_specs=(inside, inside),
        scratch_shapes=[
            vmem((TR, LEV, 32, LON), f32),
            vmem((LEV, 32, LON), f32),
            vmem((LEV, ROWS, LON), f32),
            vmem((RING, TR, HALF, LON), f32),
            vmem((RING, 40, LON), f32),
            vmem((RING, 40, LON), f32),
            vmem((RING, HALF, LON), f32),
            vmem((TR, LEV, ROWS, LON), f32),
            vmem((HALF, LON), f32),
            vmem((HALF, LON), f32),
            dma((RING,)), dma((RING,)), dma((RING,)), dma((RING,)), dma((4,)), dma((3,)), dma((3,)), dma((1,)), dma((1,)),
        ],
        compiler_params=pltpu.CompilerParams(collective_id=0, has_side_effects=True),
        cost_estimate=pl.CostEstimate(flops=100_000_000, bytes_accessed=1_000_000, transcendentals=0),
    )(tracers, courant_frac, shifts, merid)


def solution(mesh):
    return jax.shard_map(
        per_device,
        mesh=mesh,
        in_specs=(
            P(None, None, "lat", "lon"),
            P(None, "lat", "lon"),
            P(None, "lat"),
            P(None, "lat", "lon"),
        ),
        out_specs=(P(None, None, "lat", "lon"), P(None, None, "lat", "lon")),
        check_vma=False,
    )
```

```python
import functools

import jax
import jax.numpy as jnp
from jax import lax
from jax.experimental import pallas as pl
from jax.experimental.pallas import tpu as pltpu
from jax.sharding import PartitionSpec as P

TR, LEV, ROWS, LON, RING, BANDS = 4, 8, 16, 128, 16, 16
NLAT = ROWS * BANDS
HALF = 8
REACH = 3
PARTS = 2
EACH = TR // PARTS
WIDE = EACH * HALF
SIZE = WIDE + 1
MESH = pl.DeviceIdType.MESH
FAR = tuple(sorted(range(1, RING), key=lambda d: (-min(d % 8, 8 - d % 8), d)))
ORDER = tuple(z + 8 * y for z in range(8) for y in range(2))


def lanes_iota(rows):
    return lax.broadcasted_iota(jnp.int32, (rows, LON), 1)


def rows_iota(rows):
    return lax.broadcasted_iota(jnp.int32, (rows, LON), 0)


def take(values, index):
    return jnp.take_along_axis(values, index, axis=1, mode="promise_in_bounds")


def ring(index):
    return jnp.bitwise_and(index, RING - 1)


def kernel(
    q_hbm, c_hbm, s_hbm, v_hbm, upd_hbm, flux_hbm,
    s_ref, qx, mx, cv, gat, ret, back, pack, base, flux_v, cw_out, cw_in,
    s1, r1, s2, r2, sl, sh, rh, se, re, so,
):
    me = lax.axis_index("lon")
    lat = lax.axis_index("lat")

    barrier = pltpu.get_barrier_semaphore()
    for d in FAR:
        pl.semaphore_signal(barrier, inc=1, device_id={"lon": ring(me + d)}, device_id_type=MESH)
    north, south = ring(lat + 1), ring(lat + BANDS - 1)
    for peer in (north, south):
        pl.semaphore_signal(barrier, inc=1, device_id={"lat": peer}, device_id_type=MESH)

    def of_home(h, part):
        rows = pl.ds(pl.multiple_of(HALF + (h % 2) * HALF, HALF), HALF)
        return qx.at[pl.ds(part * EACH, EACH), h // 2, rows, :]

    own_q = pltpu.make_async_copy(q_hbm, qx.at[:, :, pl.ds(8, ROWS), :], sl.at[0])
    own_s = pltpu.make_async_copy(s_hbm, s_ref, sl.at[1])
    own_c = pltpu.make_async_copy(c_hbm, cv, sl.at[2])
    own_v = pltpu.make_async_copy(v_hbm, mx.at[:, pl.ds(8, ROWS), :], sl.at[3])
    for copy in (own_q, own_s, own_c, own_v):
        copy.start()
    own_q.wait()
    own = [pltpu.make_async_copy(of_home(me, p), gat.at[me, pl.ds(p * EACH, EACH)], sl.at[4 + p]) for p in range(PARTS)]
    for copy in own:
        copy.start()

    lane8, row8 = lanes_iota(HALF), rows_iota(HALF)
    own_s.wait()
    line = s_ref[pl.ds(me // 2, 1), :].astype(jnp.float32)
    pick = lax.broadcasted_iota(jnp.int32, (HALF, ROWS), 1) == (
        lax.broadcasted_iota(jnp.int32, (HALF, ROWS), 0) + HALF * (me % 2)
    )
    shift = jnp.sum(jnp.where(pick, jnp.broadcast_to(line, (HALF, ROWS)), 0.0), axis=1, keepdims=True)
    first = -1 - jnp.broadcast_to(shift, (HALF, LON)).astype(jnp.int32)
    raised = first + REACH * LON
    low = jnp.right_shift(raised, 7)
    remain = jnp.bitwise_and(raised, LON - 1)
    hop = jnp.where(lane8 >= remain, low, low + 1)
    bits = [jnp.bitwise_and(hop, 1 << n) != 0 for n in range(3)]
    turn = jnp.bitwise_and(lane8 + remain, LON - 1)
    signs = []
    for off in range(-REACH, REACH):
        cell = off * LON + lane8
        if off < 0:
            signs.append(jnp.where(cell >= first, -1.0, 0.0))
        else:
            signs.append(jnp.where(cell < first, 1.0, 0.0))
    group = lane8 // WIDE
    ends = jnp.where(group == 0, LON - 1, jnp.where(group == 1, 0, 1))

    own_c.wait()
    packed = jnp.zeros((HALF, LON), jnp.float32)
    for tile in range(2 * LEV):
        column = cv[tile // 2, HALF * (tile % 2) : HALF * (tile % 2) + HALF, LON - 1 : LON]
        packed = jnp.where(lane8 == HALF * tile + row8, column, packed)
    cw_out[...] = jnp.broadcast_to(jnp.sum(packed, axis=0, keepdims=True), (HALF, LON))

    pl.semaphore_wait(barrier, RING + 1)

    def gather_copy(d, part):
        target = ring(me + d)
        return pltpu.make_async_remote_copy(
            of_home(target, part), gat.at[me, pl.ds(part * EACH, EACH)], s1.at[part, d], r1.at[part, d],
            device_id={"lon": target}, device_id_type=MESH,
        )

    for part in range(PARTS):
        for d in FAR:
            gather_copy(d, part).start()

    halo = [
        (q_hbm.at[:, :, pl.ds(ROWS - 2, 2), :], qx.at[:, :, pl.ds(6, 2), :], north),
        (q_hbm.at[:, :, pl.ds(0, 2), :], qx.at[:, :, pl.ds(24, 2), :], south),
        (v_hbm.at[:, pl.ds(ROWS - 1, 1), :], mx.at[:, pl.ds(7, 1), :], north),
    ]
    halo = [
        pltpu.make_async_remote_copy(a, b, sh.at[i], rh.at[i], device_id={"lat": p}, device_id_type=MESH)
        for i, (a, b, p) in enumerate(halo)
    ]
    for copy in halo:
        copy.start()
    edge = pltpu.make_async_remote_copy(
        cw_out, cw_in, se.at[0], re.at[0], device_id={"lon": ring(me + 1)}, device_id_type=MESH
    )
    edge.start()

    own_v.wait()
    for copy in halo:
        copy.wait_recv()
    face = lat * ROWS + rows_iota(ROWS)

    def meridional(l, carry):
        for o in (-1, 0):
            v = mx[l, 8 + o : 24 + o]
            v = jnp.where((face + o == NLAT - 1) | (face + o < 0), 0.0, v)
            up = v >= 0.0
            half_low = v * (1.0 - v) * 0.5
            half_high = v * (1.0 + v) * 0.5
            zero_low = (face + o <= 0) | (face + o >= NLAT - 1)
            zero_high = (face + o + 1 <= 0) | (face + o + 1 >= NLAT - 1)
            for tr in range(TR):
                q_low = qx[tr, l, 8 + o : 24 + o]
                q_high = qx[tr, l, 9 + o : 25 + o]
                side_low = jnp.where(zero_low, 0.0, 0.5 * (q_high - qx[tr, l, 7 + o : 23 + o]))
                side_high = jnp.where(zero_high, 0.0, 0.5 * (qx[tr, l, 10 + o : 26 + o] - q_low))
                flux = jnp.where(up, v * q_low + half_low * side_low, v * q_high - half_high * side_high)
                if o < 0:
                    base[tr, l] = qx[tr, l, 8:24] + flux
                else:
                    base[tr, l] = base[tr, l] - flux
        return carry

    lax.fori_loop(0, LEV, meridional, 0)

    def return_copy(t, part):
        return pltpu.make_async_remote_copy(
            ret.at[part, t, pl.ds(0, SIZE)], back.at[part, me, pl.ds(0, SIZE)], s2.at[part, t], r2.at[part, me],
            device_id={"lon": t}, device_id_type=MESH,
        )

    for part in range(PARTS):
        own[part].wait()
        for d in FAR[::-1]:
            gather_copy(d, part).wait_recv()

        rows_of = []
        for i in range(EACH):
            tr = part * EACH + i
            blocks = [gat[b, tr] for b in range(RING)]
            mine = ((lane8 // HALF) % EACH == i) & (lane8 % HALF == row8)
            one = [jnp.where(bits[0], blocks[(b - 2) % RING], blocks[(b - 3) % RING]) for b in range(RING)]
            two = [jnp.where(bits[1], one[(b + 2) % RING], one[b]) for b in range(RING)]
            aligned = [take(jnp.where(bits[2], two[(b + 4) % RING], two[b]), turn) for b in range(RING)]
            tips = [take(a, ends) for a in aligned]
            for b in range(RING):
                ret[part, b, HALF * i : HALF * i + HALF, :] = aligned[b]
                total = blocks[(b - REACH) % RING] * signs[0]
                for n in range(1, 2 * REACH):
                    total = total + blocks[(b - REACH + n) % RING] * signs[n]
                offset = jnp.sum(total, axis=1, keepdims=True)
                extra = jnp.where(group == 0, tips[b - 1], jnp.where(group == 3, offset, tips[(b + 1) % RING]))
                if i == 0:
                    pack[b] = jnp.where(mine, extra, 0.0)
                else:
                    pack[b] = jnp.where(mine, extra, pack[b])
        for b in range(RING):
            ret[part, b, WIDE:SIZE, :] = jnp.sum(pack[b], axis=0, keepdims=True)

        for t in ORDER:
            @pl.when(t != me)
            def _():
                return_copy(t, part).start()

        pltpu.make_async_copy(
            ret.at[part, me, pl.ds(0, SIZE)], back.at[part, me, pl.ds(0, SIZE)], r2.at[part, me]
        ).start()

    edge.wait_recv()
    west_row = jnp.broadcast_to(cw_in[0:1, :], (HALF, LON))
    upper = jnp.where(
        lax.broadcasted_iota(jnp.int32, (LON, LON), 0) <= lax.broadcasted_iota(jnp.int32, (LON, LON), 1), 1.0, 0.0
    ).astype(jnp.bfloat16)
    rows = 4 * WIDE
    lane, row = lanes_iota(rows), rows_iota(rows) % WIDE
    index_a = jnp.where(lane == LON - 2, 1, jnp.where(lane == LON - 1, 2, 0)) * WIDE + row
    index_b = jnp.where(lane == LON - 1, 1, 3) * WIDE + row

    def finish(part, d):
        past = jnp.where(d == 4, 4, 0)
        homes = [ring(me + d), ring(me + RING - d), ring(me + 8 + d + past), ring(me + 8 - d + past)]
        places = [(h // 2, pl.multiple_of((h % 2) * HALF, HALF)) for h in homes]
        for h in homes:
            pltpu.make_async_copy(
                ret.at[part, h, pl.ds(0, SIZE)], back.at[part, h, pl.ds(0, SIZE)], r2.at[part, h]
            ).wait()
        cells = jnp.concatenate([back[part, h, 0:WIDE] for h in homes], axis=0)
        extra = jnp.concatenate(
            [jnp.broadcast_to(back[part, h, WIDE:SIZE], (WIDE, LON)) for h in homes], axis=0
        )
        ext_a, ext_b = take(extra, index_a), take(extra, index_b)
        plus1 = jnp.where(lane == LON - 1, ext_b, pltpu.roll(cells, LON - 1, 1))
        plus2 = jnp.where(lane >= LON - 2, ext_a, pltpu.roll(cells, LON - 2, 1))
        q = jnp.concatenate(
            [qx[part * EACH + i, l, pl.ds(start + 8, HALF), :] for l, start in places for i in range(EACH)], axis=0
        )
        diff = q - cells
        part0 = diff.astype(jnp.bfloat16)
        rest = diff - part0.astype(jnp.float32)
        part1 = rest.astype(jnp.bfloat16)
        part2 = (rest - part1.astype(jnp.float32)).astype(jnp.bfloat16)
        sums = (
            jnp.dot(part2, upper, preferred_element_type=jnp.float32)
            + jnp.dot(part1, upper, preferred_element_type=jnp.float32)
        ) + jnp.dot(part0, upper, preferred_element_type=jnp.float32)
        frac = [cv[l, pl.ds(start, HALF), :] for l, start in places]
        west = [take(west_row, HALF * h + row8) for h in homes]
        weights = []
        for c in (frac, west):
            t = [1.0 - x for x in c]
            tt = [(x * x - x) * 0.25 for x in t]
            for w in (t, tt):
                weights.append(jnp.concatenate([x for x in w for _ in range(EACH)], axis=0))
        t, tt, t_west, tt_west = weights
        offset = jnp.broadcast_to(ext_b[:, 0:1], (rows, LON))
        flux = sums - offset - (plus1 * t + (plus2 - cells) * tt)
        first_west = -ext_b - (cells * t_west + (plus1 - ext_a) * tt_west)
        flux_west = jnp.where(lane == 0, first_west, pltpu.roll(flux, 1, 1))
        change = flux - flux_west
        at = 0
        for l, start in places:
            for i in range(EACH):
                spot = (part * EACH + i, l, pl.ds(start, HALF), slice(None))
                flux_v[spot] = flux[at : at + HALF]
                base[spot] = base[spot] - change[at : at + HALF]
                at += HALF

    written = []
    for part in range(PARTS):
        def step(d, carry):
            finish(part, d)
            return carry

        lax.fori_loop(1, 5, step, 0)
        some = pl.ds(part * EACH, EACH)
        for i, (src, dst) in enumerate(((flux_v, flux_hbm), (base, upd_hbm))):
            copy = pltpu.make_async_copy(src.at[some], dst.at[some], so.at[part, i])
            copy.start()
            written.append(copy)

    for part in range(PARTS):
        for d in FAR:
            gather_copy(d, part).wait_send()
        for t in ORDER:
            @pl.when(t != me)
            def _():
                return_copy(t, part).wait_send()
    for copy in halo:
        copy.wait_send()
    edge.wait_send()
    for copy in written:
        copy.wait()


def hand_on(upd_in, flux_in, upd_out, flux_out, upd_v, flux_v, arrived, gone):
    legs = []
    for i, (src, mid, dst) in enumerate(((upd_in, upd_v, upd_out), (flux_in, flux_v, flux_out))):
        for tr in range(TR):
            legs.append((
                pltpu.make_async_copy(src.at[tr], mid.at[tr], arrived.at[i, tr]),
                pltpu.make_async_copy(mid.at[tr], dst.at[tr], gone.at[i, tr]),
            ))
    for first, _ in legs:
        first.start()
    for first, second in legs:
        first.wait()
        second.start()
    for _, second in legs:
        second.wait()


def per_device(tracers, courant_frac, shifts, merid):
    vmem, dma, f32 = pltpu.VMEM, pltpu.SemaphoreType.DMA, jnp.float32
    shape = jax.ShapeDtypeStruct((TR, LEV, ROWS, LON), f32)
    anywhere = pl.BlockSpec(memory_space=pl.ANY)
    tall = -(-SIZE // 8) * 8
    updated, flux = pl.pallas_call(
        kernel,
        out_shape=(shape, shape),
        in_specs=[anywhere] * 4,
        out_specs=(anywhere, anywhere),
        scratch_shapes=[
            vmem((LEV, ROWS), jnp.int32),
            vmem((TR, LEV, 32, LON), f32),
            vmem((LEV, 32, LON), f32),
            vmem((LEV, ROWS, LON), f32),
            vmem((RING, TR, HALF, LON), f32),
            vmem((PARTS, RING, tall, LON), f32),
            vmem((PARTS, RING, tall, LON), f32),
            vmem((RING, HALF, LON), f32),
            vmem((TR, LEV, ROWS, LON), f32),
            vmem((TR, LEV, ROWS, LON), f32),
            vmem((HALF, LON), f32),
            vmem((HALF, LON), f32),
            dma((PARTS, RING)), dma((PARTS, RING)), dma((PARTS, RING)), dma((PARTS, RING)),
            dma((4 + PARTS,)), dma((3,)), dma((3,)), dma((1,)), dma((1,)), dma((PARTS, 2)),
        ],
        compiler_params=pltpu.CompilerParams(collective_id=0, has_side_effects=True),
        cost_estimate=pl.CostEstimate(flops=100_000_000, bytes_accessed=1_000_000, transcendentals=0),
    )(tracers, courant_frac, shifts, merid)
    whole = vmem((TR, LEV, ROWS, LON), f32)
    return pl.pallas_call(
        hand_on,
        out_shape=(shape, shape),
        in_specs=[anywhere] * 2,
        out_specs=(anywhere, anywhere),
        scratch_shapes=[whole, whole, dma((2, TR)), dma((2, TR))],
        cost_estimate=pl.CostEstimate(flops=0, bytes_accessed=2_000_000, transcendentals=0),
    )(updated, flux)


def solution(mesh):
    return jax.shard_map(
        per_device,
        mesh=mesh,
        in_specs=(
            P(None, None, "lat", "lon"),
            P(None, "lat", "lon"),
            P(None, "lat"),
            P(None, "lat", "lon"),
        ),
        out_specs=(P(None, None, "lat", "lon"), P(None, None, "lat", "lon")),
        check_vma=False,
    )
```

```python
import functools

import jax
import jax.numpy as jnp
from jax import lax
from jax.experimental import pallas as pl
from jax.experimental.pallas import tpu as pltpu
from jax.sharding import PartitionSpec as P

TR, LEV, ROWS, LON, RING, BANDS = 4, 8, 16, 128, 16, 16
NLAT = ROWS * BANDS
HALF = 8
REACH = 3
PARTS = 2
EACH = TR // PARTS
WIDE = EACH * HALF
SIZE = WIDE + 1
MESH = pl.DeviceIdType.MESH
FAR = tuple(sorted(range(RING), key=lambda d: (-min(d % 8, 8 - d % 8), d)))
ORDER = (0, 8, 9, 1, 2, 10, 3, 11, 7, 15, 6, 14, 4, 12, 5, 13)


def lanes_iota(rows):
    return lax.broadcasted_iota(jnp.int32, (rows, LON), 1)


def rows_iota(rows):
    return lax.broadcasted_iota(jnp.int32, (rows, LON), 0)


def take(values, index):
    return jnp.take_along_axis(values, index, axis=1, mode="promise_in_bounds")


def ring(index):
    return jnp.bitwise_and(index, RING - 1)


def kernel(
    q_hbm, c_hbm, s_hbm, v_hbm, base, flux_v,
    s_ref, qx, mx, cv, gat, ret, back, pack, cw_out, cw_in,
    s1, r1, s2, r2, sl, sh, rh, se, re,
):
    me = lax.axis_index("lon")
    lat = lax.axis_index("lat")

    barrier = pltpu.get_barrier_semaphore()
    pair = jnp.bitwise_xor(lat, 1)
    north, south = ring(lat + 1), ring(lat + BANDS - 1)
    other = north + south - pair
    for d in FAR:
        pl.semaphore_signal(barrier, inc=1, device_id={"lon": ring(me + d), "lat": pair}, device_id_type=MESH)
    pl.semaphore_signal(barrier, inc=1, device_id={"lat": other}, device_id_type=MESH)
    pl.semaphore_signal(barrier, inc=1, device_id={"lon": ring(me + RING - 1)}, device_id_type=MESH)

    def of_home(h, part):
        rows = pl.ds(pl.multiple_of(HALF + (h % 2) * HALF, HALF), HALF)
        return qx.at[pl.ds(part * EACH, EACH), h // 2, rows, :]

    own_q = pltpu.make_async_copy(q_hbm, qx.at[:, :, pl.ds(8, ROWS), :], sl.at[0])
    own_c = pltpu.make_async_copy(c_hbm, cv, sl.at[2])
    own_v = pltpu.make_async_copy(v_hbm, mx.at[:, pl.ds(8, ROWS), :], sl.at[3])
    for copy in (own_q, own_c, own_v):
        copy.start()

    lane8, row8 = lanes_iota(HALF), rows_iota(HALF)
    own_c.wait()
    packed = jnp.zeros((HALF, LON), jnp.float32)
    for tile in range(2 * LEV):
        column = cv[tile // 2, HALF * (tile % 2) : HALF * (tile % 2) + HALF, LON - 1 : LON]
        packed = jnp.where(lane8 == HALF * tile + row8, column, packed)
    cw_out[...] = jnp.broadcast_to(jnp.sum(packed, axis=0, keepdims=True), (HALF, LON))

    own_q.wait()
    pl.semaphore_wait(barrier, RING + 2)

    def gather_copy(d, part):
        target = ring(me + d)
        return pltpu.make_async_remote_copy(
            of_home(target, part), gat.at[part, me], s1.at[part], r1.at[part],
            device_id={"lon": target, "lat": pair}, device_id_type=MESH,
        )

    for part in range(PARTS):
        for d in FAR:
            gather_copy(d, part).start()

    steps = pltpu.make_async_remote_copy(
        s_hbm, s_ref, se.at[1], re.at[1], device_id={"lat": pair}, device_id_type=MESH
    )
    steps.start()

    halo = [
        (q_hbm.at[:, :, pl.ds(ROWS - 2, 2), :], qx.at[:, :, pl.ds(6, 2), :], north),
        (q_hbm.at[:, :, pl.ds(0, 2), :], qx.at[:, :, pl.ds(24, 2), :], south),
        (v_hbm.at[:, pl.ds(ROWS - 1, 1), :], mx.at[:, pl.ds(7, 1), :], north),
    ]
    halo = [
        pltpu.make_async_remote_copy(a, b, sh.at[i], rh.at[i], device_id={"lat": p}, device_id_type=MESH)
        for i, (a, b, p) in enumerate(halo)
    ]
    for copy in halo:
        copy.start()
    edge = pltpu.make_async_remote_copy(
        cw_out, cw_in, se.at[0], re.at[0], device_id={"lon": ring(me + 1)}, device_id_type=MESH
    )
    edge.start()

    steps.wait_recv()
    line = s_ref[pl.ds(me // 2, 1), :].astype(jnp.float32)
    pick = lax.broadcasted_iota(jnp.int32, (HALF, ROWS), 1) == (
        lax.broadcasted_iota(jnp.int32, (HALF, ROWS), 0) + HALF * (me % 2)
    )
    shift = jnp.sum(jnp.where(pick, jnp.broadcast_to(line, (HALF, ROWS)), 0.0), axis=1, keepdims=True)
    first = -1 - jnp.broadcast_to(shift, (HALF, LON)).astype(jnp.int32)
    raised = first + REACH * LON
    low = jnp.right_shift(raised, 7)
    remain = jnp.bitwise_and(raised, LON - 1)
    hop = jnp.where(lane8 >= remain, low, low + 1)
    bits = [jnp.bitwise_and(hop, 1 << n) != 0 for n in range(3)]
    turn = jnp.bitwise_and(lane8 + remain, LON - 1)
    signs = []
    for off in range(-REACH, REACH):
        cell = off * LON + lane8
        if off < 0:
            signs.append(jnp.where(cell >= first, -1.0, 0.0))
        else:
            signs.append(jnp.where(cell < first, 1.0, 0.0))
    group = lane8 // WIDE
    ends = jnp.where(group == 0, LON - 1, jnp.where(group == 1, 0, 1))

    own_v.wait()
    for copy in halo:
        copy.wait_recv()
    face = lat * ROWS + rows_iota(ROWS)

    def meridional(l, carry):
        for o in (-1, 0):
            v = mx[l, 8 + o : 24 + o]
            v = jnp.where((face + o == NLAT - 1) | (face + o < 0), 0.0, v)
            up = v >= 0.0
            half_low = v * (1.0 - v) * 0.5
            half_high = v * (1.0 + v) * 0.5
            zero_low = (face + o <= 0) | (face + o >= NLAT - 1)
            zero_high = (face + o + 1 <= 0) | (face + o + 1 >= NLAT - 1)
            for tr in range(TR):
                q_low = qx[tr, l, 8 + o : 24 + o]
                q_high = qx[tr, l, 9 + o : 25 + o]
                side_low = jnp.where(zero_low, 0.0, 0.5 * (q_high - qx[tr, l, 7 + o : 23 + o]))
                side_high = jnp.where(zero_high, 0.0, 0.5 * (qx[tr, l, 10 + o : 26 + o] - q_low))
                flux = jnp.where(up, v * q_low + half_low * side_low, v * q_high - half_high * side_high)
                if o < 0:
                    base[tr, l] = qx[tr, l, 8:24] + flux
                else:
                    base[tr, l] = base[tr, l] - flux
        return carry

    lax.fori_loop(0, LEV, meridional, 0)

    def away(t):
        hops = jnp.bitwise_and(t - me + RING, 7)
        hops = jnp.minimum(hops, 8 - hops)
        return jnp.where(hops == 0, 3, hops - 1)

    def return_copy(t, part):
        return pltpu.make_async_remote_copy(
            ret.at[part, t, pl.ds(0, SIZE)], back.at[part, me, pl.ds(0, SIZE)], s2.at[part], r2.at[part, away(t)],
            device_id={"lon": t, "lat": pair}, device_id_type=MESH,
        )

    def take_bytes(ref, sem):
        pltpu.make_async_copy(ref, ref, sem).wait()

    for part in range(PARTS):
        take_bytes(gat.at[part], r1.at[part])
        for i in range(EACH):
            blocks = [gat[part, b, i] for b in range(RING)]
            mine = ((lane8 // HALF) % EACH == i) & (lane8 % HALF == row8)
            one = [jnp.where(bits[0], blocks[(b - 2) % RING], blocks[(b - 3) % RING]) for b in range(RING)]
            two = [jnp.where(bits[1], one[(b + 2) % RING], one[b]) for b in range(RING)]
            aligned = [take(jnp.where(bits[2], two[(b + 4) % RING], two[b]), turn) for b in range(RING)]
            tips = [take(a, ends) for a in aligned]
            for b in range(RING):
                ret[part, b, HALF * i : HALF * i + HALF, :] = aligned[b]
                total = blocks[(b - REACH) % RING] * signs[0]
                for n in range(1, 2 * REACH):
                    total = total + blocks[(b - REACH + n) % RING] * signs[n]
                offset = jnp.sum(total, axis=1, keepdims=True)
                extra = jnp.where(group == 0, tips[b - 1], jnp.where(group == 3, offset, tips[(b + 1) % RING]))
                if i == 0:
                    pack[b] = jnp.where(mine, extra, 0.0)
                else:
                    pack[b] = jnp.where(mine, extra, pack[b])
        for b in range(RING):
            ret[part, b, WIDE:SIZE, :] = jnp.sum(pack[b], axis=0, keepdims=True)

        for t in ORDER:
            return_copy(t, part).start()

    edge.wait_recv()
    west_row = jnp.broadcast_to(cw_in[0:1, :], (HALF, LON))
    upper = jnp.where(
        lax.broadcasted_iota(jnp.int32, (LON, LON), 0) <= lax.broadcasted_iota(jnp.int32, (LON, LON), 1), 1.0, 0.0
    ).astype(jnp.bfloat16)
    rows = 4 * WIDE
    lane, row = lanes_iota(rows), rows_iota(rows) % WIDE
    index_a = jnp.where(lane == LON - 2, 1, jnp.where(lane == LON - 1, 2, 0)) * WIDE + row
    index_b = jnp.where(lane == LON - 1, 1, 3) * WIDE + row

    def finish(part, d):
        past = jnp.where(d == 4, 4, 0)
        homes = [ring(me + d), ring(me + RING - d), ring(me + 8 + d + past), ring(me + 8 - d + past)]
        places = [(h // 2, pl.multiple_of((h % 2) * HALF, HALF)) for h in homes]
        take_bytes(back.at[part, pl.ds(0, 4), pl.ds(0, SIZE)], r2.at[part, d - 1])
        cells = jnp.concatenate([back[part, h, 0:WIDE] for h in homes], axis=0)
        extra = jnp.concatenate(
            [jnp.broadcast_to(back[part, h, WIDE:SIZE], (WIDE, LON)) for h in homes], axis=0
        )
        ext_a, ext_b = take(extra, index_a), take(extra, index_b)
        plus1 = jnp.where(lane == LON - 1, ext_b, pltpu.roll(cells, LON - 1, 1))
        plus2 = jnp.where(lane >= LON - 2, ext_a, pltpu.roll(cells, LON - 2, 1))
        q = jnp.concatenate(
            [qx[part * EACH + i, l, pl.ds(start + 8, HALF), :] for l, start in places for i in range(EACH)], axis=0
        )
        diff = q - cells
        part0 = diff.astype(jnp.bfloat16)
        rest = diff - part0.astype(jnp.float32)
        part1 = rest.astype(jnp.bfloat16)
        part2 = (rest - part1.astype(jnp.float32)).astype(jnp.bfloat16)
        sums = (
            jnp.dot(part2, upper, preferred_element_type=jnp.float32)
            + jnp.dot(part1, upper, preferred_element_type=jnp.float32)
        ) + jnp.dot(part0, upper, preferred_element_type=jnp.float32)
        frac = [cv[l, pl.ds(start, HALF), :] for l, start in places]
        west = [take(west_row, HALF * h + row8) for h in homes]
        weights = []
        for c in (frac, west):
            t = [1.0 - x for x in c]
            tt = [(x * x - x) * 0.25 for x in t]
            for w in (t, tt):
                weights.append(jnp.concatenate([x for x in w for _ in range(EACH)], axis=0))
        t, tt, t_west, tt_west = weights
        offset = jnp.broadcast_to(ext_b[:, 0:1], (rows, LON))
        flux = sums - offset - (plus1 * t + (plus2 - cells) * tt)
        first_west = -ext_b - (cells * t_west + (plus1 - ext_a) * tt_west)
        flux_west = jnp.where(lane == 0, first_west, pltpu.roll(flux, 1, 1))
        change = flux - flux_west
        at = 0
        for l, start in places:
            for i in range(EACH):
                spot = (part * EACH + i, l, pl.ds(start, HALF), slice(None))
                flux_v[spot] = flux[at : at + HALF]
                base[spot] = base[spot] - change[at : at + HALF]
                at += HALF

    for part in range(PARTS):
        def step(d, carry):
            finish(part, d)
            return carry

        lax.fori_loop(1, 5, step, 0)

    for part in range(PARTS):
        take_bytes(gat.at[part], s1.at[part])
        take_bytes(back.at[part, :, pl.ds(0, SIZE)], s2.at[part])
    for copy in halo:
        copy.wait_send()
    edge.wait_send()
    steps.wait_send()


def hand_on(upd_in, flux_in, upd_out, flux_out, gone):
    legs = [
        pltpu.make_async_copy(src, dst, gone.at[i])
        for i, (src, dst) in enumerate(((upd_in, upd_out), (flux_in, flux_out)))
    ]
    for leg in legs:
        leg.start()
    for leg in legs:
        leg.wait()


def per_device(tracers, courant_frac, shifts, merid):
    vmem, dma, f32 = pltpu.VMEM, pltpu.SemaphoreType.DMA, jnp.float32
    shape = jax.ShapeDtypeStruct((TR, LEV, ROWS, LON), f32)
    anywhere = pl.BlockSpec(memory_space=pl.ANY)
    tall = -(-SIZE // 8) * 8
    held = pltpu.VMEM((TR, LEV, ROWS, LON), f32)
    inside = pl.BlockSpec(memory_space=pltpu.VMEM)
    inputs = [pltpu.with_memory_space_constraint(x, pltpu.HBM) for x in (tracers, courant_frac, shifts, merid)]
    updated, flux = pl.pallas_call(
        kernel,
        out_shape=(held, held),
        in_specs=[pl.BlockSpec(memory_space=pltpu.HBM)] * 4,
        out_specs=(inside, inside),
        scratch_shapes=[
            vmem((LEV, ROWS), jnp.int32),
            vmem((TR, LEV, 32, LON), f32),
            vmem((LEV, 32, LON), f32),
            vmem((LEV, ROWS, LON), f32),
            vmem((PARTS, RING, EACH, HALF, LON), f32),
            vmem((PARTS, RING, tall, LON), f32),
            vmem((PARTS, RING, tall, LON), f32),
            vmem((RING, HALF, LON), f32),
            vmem((HALF, LON), f32),
            vmem((HALF, LON), f32),
            dma((PARTS,)), dma((PARTS,)), dma((PARTS,)), dma((PARTS, 4)),
            dma((4,)), dma((3,)), dma((3,)), dma((2,)), dma((2,)),
        ],
        compiler_params=pltpu.CompilerParams(collective_id=0, has_side_effects=True, vmem_limit_bytes=16 * 2**20),
        cost_estimate=pl.CostEstimate(flops=100_000_000, bytes_accessed=1_000_000, transcendentals=0),
    )(*inputs)
    return pl.pallas_call(
        hand_on,
        out_shape=(shape, shape),
        in_specs=[inside] * 2,
        out_specs=(anywhere, anywhere),
        scratch_shapes=[dma((2,))],
        compiler_params=pltpu.CompilerParams(vmem_limit_bytes=2**20),
        cost_estimate=pl.CostEstimate(flops=0, bytes_accessed=1_000_000, transcendentals=0),
    )(*(pltpu.with_memory_space_constraint(x, pltpu.VMEM) for x in (updated, flux)))


def solution(mesh):
    return jax.shard_map(
        per_device,
        mesh=mesh,
        in_specs=(
            P(None, None, "lat", "lon"),
            P(None, "lat", "lon"),
            P(None, "lat"),
            P(None, "lat", "lon"),
        ),
        out_specs=(P(None, None, "lat", "lon"), P(None, None, "lat", "lon")),
        check_vma=False,
    )
```

```python
import functools

import jax
import jax.numpy as jnp
from jax import lax
from jax.experimental import pallas as pl
from jax.experimental.pallas import tpu as pltpu
from jax.sharding import PartitionSpec as P

TR, LEV, ROWS, LON, RING, BANDS = 4, 8, 16, 128, 16, 16
NLAT = ROWS * BANDS
HALF = 8
REACH = 3
PARTS = 2
EACH = TR // PARTS
WIDE = EACH * HALF
SIZE = WIDE + 1
FIN = PARTS // 2
MESH = pl.DeviceIdType.MESH
FAR = tuple(sorted(range(1, RING), key=lambda d: (-min(d % 8, 8 - d % 8), d)))
ORDER = (0, 8, 9, 1, 2, 10, 3, 11, 7, 15, 6, 14, 4, 12, 5, 13)


def lanes_iota(rows):
    return lax.broadcasted_iota(jnp.int32, (rows, LON), 1)


def rows_iota(rows):
    return lax.broadcasted_iota(jnp.int32, (rows, LON), 0)


def take(values, index):
    return jnp.take_along_axis(values, index, axis=1, mode="promise_in_bounds")


def ring(index):
    return jnp.bitwise_and(index, RING - 1)


def kernel(
    q_hbm, c_hbm, s_hbm, v_hbm, base, flux_v,
    s_ref, qx, mx, cv, gat, ret, back, pack, cw_out, cw_in,
    s1, r1, s2, r2, sl, sh, rh, se, re,
):
    me = lax.axis_index("lon")
    lat = lax.axis_index("lat")

    barrier = pltpu.get_barrier_semaphore()
    north, south = ring(lat + 1), ring(lat + BANDS - 1)
    for d in FAR:
        pl.semaphore_signal(barrier, inc=1, device_id={"lon": ring(me + d)}, device_id_type=MESH)
    for peer in (north, south):
        pl.semaphore_signal(barrier, inc=1, device_id={"lat": peer}, device_id_type=MESH)

    def of_home(h, tr):
        return qx.at[tr, h // 2, pl.ds(pl.multiple_of(HALF + (h % 2) * HALF, HALF), HALF), :]

    own_q = pltpu.make_async_copy(q_hbm, qx.at[:, :, pl.ds(8, ROWS), :], sl.at[0])
    own_c = pltpu.make_async_copy(c_hbm, cv, sl.at[2])
    own_v = pltpu.make_async_copy(v_hbm, mx.at[:, pl.ds(8, ROWS), :], sl.at[3])
    own_s = pltpu.make_async_copy(s_hbm, s_ref, sl.at[1])
    for copy in (own_q, own_s, own_c, own_v):
        copy.start()

    lane8, row8 = lanes_iota(HALF), rows_iota(HALF)
    own_c.wait()
    packed = jnp.zeros((HALF, LON), jnp.float32)
    for tile in range(2 * LEV):
        column = cv[tile // 2, HALF * (tile % 2) : HALF * (tile % 2) + HALF, LON - 1 : LON]
        packed = jnp.where(lane8 == HALF * tile + row8, column, packed)
    cw_out[...] = jnp.broadcast_to(jnp.sum(packed, axis=0, keepdims=True), (HALF, LON))

    own_q.wait()
    pl.semaphore_wait(barrier, RING + 1)

    def gather_copy(d, tr):
        target = ring(me + d)
        return pltpu.make_async_remote_copy(
            of_home(target, tr), gat.at[tr, me], s1.at[tr], r1.at[tr],
            device_id={"lon": target}, device_id_type=MESH,
        )

    for tr in range(TR):
        for d in FAR:
            gather_copy(d, tr).start()
        pltpu.make_async_copy(of_home(me, tr), gat.at[tr, me], r1.at[tr]).start()

    halo = [
        (q_hbm.at[:, :, pl.ds(ROWS - 2, 2), :], qx.at[:, :, pl.ds(6, 2), :], north),
        (q_hbm.at[:, :, pl.ds(0, 2), :], qx.at[:, :, pl.ds(24, 2), :], south),
        (v_hbm.at[:, pl.ds(ROWS - 1, 1), :], mx.at[:, pl.ds(7, 1), :], north),
    ]
    halo = [
        pltpu.make_async_remote_copy(a, b, sh.at[i], rh.at[i], device_id={"lat": p}, device_id_type=MESH)
        for i, (a, b, p) in enumerate(halo)
    ]
    for copy in halo:
        copy.start()
    edge = pltpu.make_async_remote_copy(
        cw_out, cw_in, se.at[0], re.at[0], device_id={"lon": ring(me + 1)}, device_id_type=MESH
    )
    edge.start()

    own_s.wait()
    line = s_ref[pl.ds(me // 2, 1), :].astype(jnp.float32)
    pick = lax.broadcasted_iota(jnp.int32, (HALF, ROWS), 1) == (
        lax.broadcasted_iota(jnp.int32, (HALF, ROWS), 0) + HALF * (me % 2)
    )
    shift = jnp.sum(jnp.where(pick, jnp.broadcast_to(line, (HALF, ROWS)), 0.0), axis=1, keepdims=True)
    first = -1 - jnp.broadcast_to(shift, (HALF, LON)).astype(jnp.int32)
    raised = first + REACH * LON
    low = jnp.right_shift(raised, 7)
    remain = jnp.bitwise_and(raised, LON - 1)
    hop = jnp.where(lane8 >= remain, low, low + 1)
    bits = [jnp.bitwise_and(hop, 1 << n) != 0 for n in range(3)]
    turn = jnp.bitwise_and(lane8 + remain, LON - 1)
    signs = []
    for off in range(-REACH, REACH):
        cell = off * LON + lane8
        if off < 0:
            signs.append(jnp.where(cell >= first, -1.0, 0.0))
        else:
            signs.append(jnp.where(cell < first, 1.0, 0.0))
    group = lane8 // WIDE
    ends = jnp.where(group == 0, LON - 1, jnp.where(group == 1, 0, 1))

    def away(t):
        hops = jnp.bitwise_and(t - me + RING, 7)
        hops = jnp.minimum(hops, 8 - hops)
        return jnp.where(hops == 0, 3, hops - 1)

    def return_copy(t, part, rows):
        return pltpu.make_async_remote_copy(
            ret.at[part, t, rows], back.at[part, me, rows], s2.at[part], r2.at[part, away(t)],
            device_id={"lon": t}, device_id_type=MESH,
        )

    def send_back(part, rows):
        for t in ORDER:
            @pl.when(t != me)
            def _():
                return_copy(t, part, rows).start()

        pltpu.make_async_copy(ret.at[part, me, rows], back.at[part, me, rows], r2.at[part, away(me)]).start()

    def take_bytes(ref, sem):
        pltpu.make_async_copy(ref, ref, sem).wait()

    for part in range(PARTS):
        for i in range(EACH):
            tr = part * EACH + i
            take_bytes(gat.at[tr], r1.at[tr])
            blocks = [gat[tr, b] for b in range(RING)]
            mine = ((lane8 // HALF) % EACH == i) & (lane8 % HALF == row8)
            one = [jnp.where(bits[0], blocks[(b - 2) % RING], blocks[(b - 3) % RING]) for b in range(RING)]
            two = [jnp.where(bits[1], one[(b + 2) % RING], one[b]) for b in range(RING)]
            aligned = [take(jnp.where(bits[2], two[(b + 4) % RING], two[b]), turn) for b in range(RING)]
            tips = [take(a, ends) for a in aligned]
            for b in range(RING):
                ret[part, b, HALF * i : HALF * i + HALF, :] = aligned[b]
                total = blocks[(b - REACH) % RING] * signs[0]
                for n in range(1, 2 * REACH):
                    total = total + blocks[(b - REACH + n) % RING] * signs[n]
                offset = jnp.sum(total, axis=1, keepdims=True)
                extra = jnp.where(group == 0, tips[b - 1], jnp.where(group == 3, offset, tips[(b + 1) % RING]))
                if i == 0:
                    pack[b] = jnp.where(mine, extra, 0.0)
                else:
                    pack[b] = jnp.where(mine, extra, pack[b])
            if i < EACH - 1:
                send_back(part, pl.ds(HALF * i, HALF))
        for b in range(RING):
            ret[part, b, WIDE:SIZE, :] = jnp.sum(pack[b], axis=0, keepdims=True)

        send_back(part, pl.ds(WIDE - HALF, HALF + 1))

    own_v.wait()
    for copy in halo:
        copy.wait_recv()
    face = lat * ROWS + rows_iota(ROWS)

    def meridional(l, carry):
        for o in (-1, 0):
            v = mx[l, 8 + o : 24 + o]
            v = jnp.where((face + o == NLAT - 1) | (face + o < 0), 0.0, v)
            up = v >= 0.0
            half_low = v * (1.0 - v) * 0.5
            half_high = v * (1.0 + v) * 0.5
            zero_low = (face + o <= 0) | (face + o >= NLAT - 1)
            zero_high = (face + o + 1 <= 0) | (face + o + 1 >= NLAT - 1)
            for tr in range(TR):
                q_low = qx[tr, l, 8 + o : 24 + o]
                q_high = qx[tr, l, 9 + o : 25 + o]
                side_low = jnp.where(zero_low, 0.0, 0.5 * (q_high - qx[tr, l, 7 + o : 23 + o]))
                side_high = jnp.where(zero_high, 0.0, 0.5 * (qx[tr, l, 10 + o : 26 + o] - q_low))
                flux = jnp.where(up, v * q_low + half_low * side_low, v * q_high - half_high * side_high)
                if o < 0:
                    base[tr, l] = qx[tr, l, 8:24] + flux
                else:
                    base[tr, l] = base[tr, l] - flux
        return carry

    lax.fori_loop(0, LEV, meridional, 0)

    edge.wait_recv()
    west_row = jnp.broadcast_to(cw_in[0:1, :], (HALF, LON))
    upper = jnp.where(
        lax.broadcasted_iota(jnp.int32, (LON, LON), 0) <= lax.broadcasted_iota(jnp.int32, (LON, LON), 1), 1.0, 0.0
    ).astype(jnp.bfloat16)
    rows = 4 * FIN * WIDE
    lane, row = lanes_iota(rows), rows_iota(rows) % WIDE
    index_a = jnp.where(lane == LON - 2, 1, jnp.where(lane == LON - 1, 2, 0)) * WIDE + row
    index_b = jnp.where(lane == LON - 1, 1, 3) * WIDE + row

    def finish(parts, d):
        past = jnp.where(d == 4, 4, 0)
        homes = [ring(me + d), ring(me + RING - d), ring(me + 8 + d + past), ring(me + 8 - d + past)]
        places = [(h // 2, pl.multiple_of((h % 2) * HALF, HALF)) for h in homes]
        for part in parts:
            take_bytes(back.at[part, pl.ds(0, 4), pl.ds(0, SIZE)], r2.at[part, d - 1])
        cells = jnp.concatenate([back[part, h, 0:WIDE] for h in homes for part in parts], axis=0)
        extra = jnp.concatenate(
            [jnp.broadcast_to(back[part, h, WIDE:SIZE], (WIDE, LON)) for h in homes for part in parts], axis=0
        )
        ext_a, ext_b = take(extra, index_a), take(extra, index_b)
        plus1 = jnp.where(lane == LON - 1, ext_b, pltpu.roll(cells, LON - 1, 1))
        plus2 = jnp.where(lane >= LON - 2, ext_a, pltpu.roll(cells, LON - 2, 1))
        tracers = range(parts[0] * EACH, (parts[-1] + 1) * EACH)
        q = jnp.concatenate(
            [qx[tr, l, pl.ds(start + 8, HALF), :] for l, start in places for tr in tracers], axis=0
        )
        diff = q - cells
        part0 = diff.astype(jnp.bfloat16)
        rest = diff - part0.astype(jnp.float32)
        part1 = rest.astype(jnp.bfloat16)
        part2 = (rest - part1.astype(jnp.float32)).astype(jnp.bfloat16)
        sums = (
            jnp.dot(part2, upper, preferred_element_type=jnp.float32)
            + jnp.dot(part1, upper, preferred_element_type=jnp.float32)
        ) + jnp.dot(part0, upper, preferred_element_type=jnp.float32)
        frac = [cv[l, pl.ds(start, HALF), :] for l, start in places]
        west = [take(west_row, HALF * h + row8) for h in homes]
        weights = []
        for c in (frac, west):
            t = [1.0 - x for x in c]
            tt = [(x * x - x) * 0.25 for x in t]
            for w in (t, tt):
                weights.append(jnp.concatenate([x for x in w for _ in tracers], axis=0))
        t, tt, t_west, tt_west = weights
        offset = jnp.broadcast_to(ext_b[:, 0:1], (rows, LON))
        flux = sums - offset - (plus1 * t + (plus2 - cells) * tt)
        first_west = -ext_b - (cells * t_west + (plus1 - ext_a) * tt_west)
        flux_west = jnp.where(lane == 0, first_west, pltpu.roll(flux, 1, 1))
        change = flux - flux_west
        at = 0
        for l, start in places:
            for tr in tracers:
                spot = (tr, l, pl.ds(start, HALF), slice(None))
                flux_v[spot] = flux[at : at + HALF]
                base[spot] = base[spot] - change[at : at + HALF]
                at += HALF

    for first_part in range(0, PARTS, FIN):
        def step(d, carry):
            finish(range(first_part, first_part + FIN), d)
            return carry

        lax.fori_loop(1, 5, step, 0)

    for part in range(PARTS):
        take_bytes(back.at[part, pl.ds(0, RING - 1), pl.ds(0, SIZE)], s2.at[part])
    for tr in range(TR):
        take_bytes(gat.at[tr, pl.ds(0, RING - 1)], s1.at[tr])
    for copy in halo:
        copy.wait_send()
    edge.wait_send()


def hand_on(upd_in, flux_in, upd_out, flux_out, gone):
    legs = [
        pltpu.make_async_copy(src, dst, gone.at[i])
        for i, (src, dst) in enumerate(((upd_in, upd_out), (flux_in, flux_out)))
    ]
    for leg in legs:
        leg.start()
    for leg in legs:
        leg.wait()


def per_device(tracers, courant_frac, shifts, merid):
    vmem, dma, f32 = pltpu.VMEM, pltpu.SemaphoreType.DMA, jnp.float32
    shape = jax.ShapeDtypeStruct((TR, LEV, ROWS, LON), f32)
    anywhere = pl.BlockSpec(memory_space=pl.ANY)
    tall = -(-SIZE // 8) * 8
    held = pltpu.VMEM((TR, LEV, ROWS, LON), f32)
    inside = pl.BlockSpec(memory_space=pltpu.VMEM)
    inputs = [pltpu.with_memory_space_constraint(x, pltpu.HBM) for x in (tracers, courant_frac, shifts, merid)]
    updated, flux = pl.pallas_call(
        kernel,
        out_shape=(held, held),
        in_specs=[pl.BlockSpec(memory_space=pltpu.HBM)] * 4,
        out_specs=(inside, inside),
        scratch_shapes=[
            vmem((LEV, ROWS), jnp.int32),
            vmem((TR, LEV, 32, LON), f32),
            vmem((LEV, 32, LON), f32),
            vmem((LEV, ROWS, LON), f32),
            vmem((TR, RING, HALF, LON), f32),
            vmem((PARTS, RING, tall, LON), f32),
            vmem((PARTS, RING, tall, LON), f32),
            vmem((RING, HALF, LON), f32),
            vmem((HALF, LON), f32),
            vmem((HALF, LON), f32),
            dma((TR,)), dma((TR,)), dma((PARTS,)), dma((PARTS, 4)),
            dma((4,)), dma((3,)), dma((3,)), dma((1,)), dma((1,)),
        ],
        compiler_params=pltpu.CompilerParams(collective_id=0, has_side_effects=True, vmem_limit_bytes=16 * 2**20),
        cost_estimate=pl.CostEstimate(flops=100_000_000, bytes_accessed=1_000_000, transcendentals=0),
    )(*inputs)
    return pl.pallas_call(
        hand_on,
        out_shape=(shape, shape),
        in_specs=[inside] * 2,
        out_specs=(anywhere, anywhere),
        scratch_shapes=[dma((2,))],
        compiler_params=pltpu.CompilerParams(vmem_limit_bytes=2**20),
        cost_estimate=pl.CostEstimate(flops=0, bytes_accessed=1_000_000, transcendentals=0),
    )(*(pltpu.with_memory_space_constraint(x, pltpu.VMEM) for x in (updated, flux)))


def solution(mesh):
    return jax.shard_map(
        per_device,
        mesh=mesh,
        in_specs=(
            P(None, None, "lat", "lon"),
            P(None, "lat", "lon"),
            P(None, "lat"),
            P(None, "lat", "lon"),
        ),
        out_specs=(P(None, None, "lat", "lon"), P(None, None, "lat", "lon")),
        check_vma=False,
    )
```

```python
import functools

import jax
import jax.numpy as jnp
from jax import lax
from jax.experimental import pallas as pl
from jax.experimental.pallas import tpu as pltpu
from jax.sharding import PartitionSpec as P

TR, LEV, ROWS, LON, RING, BANDS = 4, 8, 16, 128, 16, 16
NLAT = ROWS * BANDS
HALF = 8
REACH = 3
PARTS = 2
EACH = TR // PARTS
WIDE = EACH * HALF
SIZE = WIDE + 1
FIN = PARTS // 2
MESH = pl.DeviceIdType.MESH
FAR = tuple(sorted(range(1, RING), key=lambda d: (-min(d % 8, 8 - d % 8), d)))
ORDER = (0, 8, 9, 1, 2, 10, 3, 11, 7, 15, 6, 14, 4, 12, 5, 13)


def lanes_iota(rows):
    return lax.broadcasted_iota(jnp.int32, (rows, LON), 1)


def rows_iota(rows):
    return lax.broadcasted_iota(jnp.int32, (rows, LON), 0)


def take(values, index):
    return jnp.take_along_axis(values, index, axis=1, mode="promise_in_bounds")


def ring(index):
    return jnp.bitwise_and(index, RING - 1)


def kernel(
    q_hbm, c_hbm, s_hbm, v_hbm, base, flux_v,
    s_ref, qx, mx, cv, gat, ret, back, pack, cw_out, cw_in,
    s1, r1, s2, r2, sl, sh, rh, se, re, ready,
):
    me = lax.axis_index("lon")
    lat = lax.axis_index("lat")

    own_q = pltpu.make_async_copy(q_hbm, qx.at[:, :, pl.ds(8, ROWS), :], sl.at[0])
    own_c = pltpu.make_async_copy(c_hbm, cv, sl.at[2])
    own_v = pltpu.make_async_copy(v_hbm, mx.at[:, pl.ds(8, ROWS), :], sl.at[3])
    own_s = pltpu.make_async_copy(s_hbm, s_ref, sl.at[1])
    own_q.start()

    barrier = pltpu.get_barrier_semaphore()
    north, south = ring(lat + 1), ring(lat + BANDS - 1)
    for d in FAR:
        pl.semaphore_signal(barrier, inc=1, device_id={"lon": ring(me + d)}, device_id_type=MESH)
    pl.semaphore_signal(barrier, inc=1, device_id={"lat": south}, device_id_type=MESH)

    def of_home(h, tr):
        return qx.at[tr, h // 2, pl.ds(pl.multiple_of(HALF + (h % 2) * HALF, HALF), HALF), :]

    for copy in (own_s, own_c, own_v):
        copy.start()

    lane8, row8 = lanes_iota(HALF), rows_iota(HALF)
    own_q.wait()
    pl.semaphore_wait(barrier, RING)

    def gather_copy(d, tr):
        target = ring(me + d)
        return pltpu.make_async_remote_copy(
            of_home(target, tr), gat.at[tr, me], s1.at[tr], r1.at[tr],
            device_id={"lon": target}, device_id_type=MESH,
        )

    for tr in range(TR):
        for d in FAR:
            gather_copy(d, tr).start()

    for tr in range(TR):
        pltpu.make_async_copy(of_home(me, tr), gat.at[tr, me], r1.at[tr]).start()

    halo = [
        (qx.at[:, :, pl.ds(8 + ROWS - 2, 2), :], qx.at[:, :, pl.ds(6, 2), :], north),
        (qx.at[:, :, pl.ds(8, 2), :], qx.at[:, :, pl.ds(24, 2), :], south),
        (v_hbm.at[:, pl.ds(ROWS - 1, 1), :], mx.at[:, pl.ds(7, 1), :], north),
    ]
    halo = [
        pltpu.make_async_remote_copy(a, b, sh.at[i], rh.at[i], device_id={"lat": p}, device_id_type=MESH)
        for i, (a, b, p) in enumerate(halo)
    ]
    pl.semaphore_signal(ready, inc=1, device_id={"lat": north}, device_id_type=MESH)
    halo[0].start()
    halo[2].start()
    own_c.wait()
    packed = jnp.zeros((HALF, LON), jnp.float32)
    for tile in range(2 * LEV):
        column = cv[tile // 2, HALF * (tile % 2) : HALF * (tile % 2) + HALF, LON - 1 : LON]
        packed = jnp.where(lane8 == HALF * tile + row8, column, packed)
    cw_out[...] = jnp.broadcast_to(jnp.sum(packed, axis=0, keepdims=True), (HALF, LON))
    edge = pltpu.make_async_remote_copy(
        cw_out, cw_in, se.at[0], re.at[0], device_id={"lon": ring(me + 1)}, device_id_type=MESH
    )
    edge.start()

    own_s.wait()
    line = s_ref[pl.ds(me // 2, 1), :].astype(jnp.float32)
    pick = lax.broadcasted_iota(jnp.int32, (HALF, ROWS), 1) == (
        lax.broadcasted_iota(jnp.int32, (HALF, ROWS), 0) + HALF * (me % 2)
    )
    shift = jnp.sum(jnp.where(pick, jnp.broadcast_to(line, (HALF, ROWS)), 0.0), axis=1, keepdims=True)
    first = -1 - jnp.broadcast_to(shift, (HALF, LON)).astype(jnp.int32)
    raised = first + REACH * LON
    low = jnp.right_shift(raised, 7)
    remain = jnp.bitwise_and(raised, LON - 1)
    hop = jnp.where(lane8 >= remain, low, low + 1)
    bits = [jnp.bitwise_and(hop, 1 << n) != 0 for n in range(3)]
    turn = jnp.bitwise_and(lane8 + remain, LON - 1)
    signs = []
    for off in range(-REACH, REACH):
        cell = off * LON + lane8
        if off < 0:
            signs.append(jnp.where(cell >= first, -1.0, 0.0))
        else:
            signs.append(jnp.where(cell < first, 1.0, 0.0))
    group = lane8 // WIDE
    ends = jnp.where(group == 0, LON - 1, jnp.where(group == 1, 0, 1))

    pl.semaphore_wait(ready, 1)
    halo[1].start()

    def away(t):
        hops = jnp.bitwise_and(t - me + RING, 7)
        hops = jnp.minimum(hops, 8 - hops)
        return jnp.where(hops == 0, 3, hops - 1)

    def return_copy(t, part, rows):
        return pltpu.make_async_remote_copy(
            ret.at[part, t, rows], back.at[part, me, rows], s2.at[part], r2.at[part, away(t)],
            device_id={"lon": t}, device_id_type=MESH,
        )

    def send_back(part, rows):
        for t in ORDER:
            @pl.when(t != me)
            def _():
                return_copy(t, part, rows).start()

        pltpu.make_async_copy(ret.at[part, me, rows], back.at[part, me, rows], r2.at[part, away(me)]).start()

    def take_bytes(ref, sem):
        pltpu.make_async_copy(ref, ref, sem).wait()

    for part in range(PARTS):
        for i in range(EACH):
            tr = part * EACH + i
            take_bytes(gat.at[tr], r1.at[tr])
            blocks = [gat[tr, b] for b in range(RING)]
            mine = ((lane8 // HALF) % EACH == i) & (lane8 % HALF == row8)
            one = [jnp.where(bits[0], blocks[(b - 2) % RING], blocks[(b - 3) % RING]) for b in range(RING)]
            two = [jnp.where(bits[1], one[(b + 2) % RING], one[b]) for b in range(RING)]
            aligned = [take(jnp.where(bits[2], two[(b + 4) % RING], two[b]), turn) for b in range(RING)]
            for b in range(RING):
                ret[part, b, HALF * i : HALF * i + HALF, :] = aligned[b]
            if i < EACH - 1:
                send_back(part, pl.ds(HALF * i, HALF))
            tips = [take(a, ends) for a in aligned]
            for b in range(RING):
                total = blocks[(b - REACH) % RING] * signs[0]
                for n in range(1, 2 * REACH):
                    total = total + blocks[(b - REACH + n) % RING] * signs[n]
                offset = jnp.sum(total, axis=1, keepdims=True)
                extra = jnp.where(group == 0, tips[b - 1], jnp.where(group == 3, offset, tips[(b + 1) % RING]))
                if i == 0:
                    pack[b] = jnp.where(mine, extra, 0.0)
                else:
                    pack[b] = jnp.where(mine, extra, pack[b])
        for b in range(RING):
            ret[part, b, WIDE:SIZE, :] = jnp.sum(pack[b], axis=0, keepdims=True)

        send_back(part, pl.ds(WIDE - HALF, HALF + 1))

    own_v.wait()
    for copy in halo:
        copy.wait_recv()
    face = lat * ROWS + rows_iota(ROWS)

    def meridional(l, carry):
        for o in (-1, 0):
            v = mx[l, 8 + o : 24 + o]
            v = jnp.where((face + o == NLAT - 1) | (face + o < 0), 0.0, v)
            up = v >= 0.0
            half_low = v * (1.0 - v) * 0.5
            half_high = v * (1.0 + v) * 0.5
            zero_low = (face + o <= 0) | (face + o >= NLAT - 1)
            zero_high = (face + o + 1 <= 0) | (face + o + 1 >= NLAT - 1)
            for tr in range(TR):
                q_low = qx[tr, l, 8 + o : 24 + o]
                q_high = qx[tr, l, 9 + o : 25 + o]
                side_low = jnp.where(zero_low, 0.0, 0.5 * (q_high - qx[tr, l, 7 + o : 23 + o]))
                side_high = jnp.where(zero_high, 0.0, 0.5 * (qx[tr, l, 10 + o : 26 + o] - q_low))
                flux = jnp.where(up, v * q_low + half_low * side_low, v * q_high - half_high * side_high)
                if o < 0:
                    base[tr, l] = qx[tr, l, 8:24] + flux
                else:
                    base[tr, l] = base[tr, l] - flux
        return carry

    lax.fori_loop(0, LEV, meridional, 0)

    edge.wait_recv()
    west_row = jnp.broadcast_to(cw_in[0:1, :], (HALF, LON))
    upper = jnp.where(
        lax.broadcasted_iota(jnp.int32, (LON, LON), 0) <= lax.broadcasted_iota(jnp.int32, (LON, LON), 1), 1.0, 0.0
    ).astype(jnp.bfloat16)
    rows = 4 * FIN * WIDE
    lane, row = lanes_iota(rows), rows_iota(rows) % WIDE
    index_a = jnp.where(lane == LON - 2, 1, jnp.where(lane == LON - 1, 2, 0)) * WIDE + row
    index_b = jnp.where(lane == LON - 1, 1, 3) * WIDE + row

    def finish(parts, d):
        past = jnp.where(d == 4, 4, 0)
        homes = [ring(me + d), ring(me + RING - d), ring(me + 8 + d + past), ring(me + 8 - d + past)]
        places = [(h // 2, pl.multiple_of((h % 2) * HALF, HALF)) for h in homes]
        for part in parts:
            take_bytes(back.at[part, pl.ds(0, 4), pl.ds(0, SIZE)], r2.at[part, d - 1])
        cells = jnp.concatenate([back[part, h, 0:WIDE] for h in homes for part in parts], axis=0)
        extra = jnp.concatenate(
            [jnp.broadcast_to(back[part, h, WIDE:SIZE], (WIDE, LON)) for h in homes for part in parts], axis=0
        )
        ext_a, ext_b = take(extra, index_a), take(extra, index_b)
        plus1 = jnp.where(lane == LON - 1, ext_b, pltpu.roll(cells, LON - 1, 1))
        plus2 = jnp.where(lane >= LON - 2, ext_a, pltpu.roll(cells, LON - 2, 1))
        tracers = range(parts[0] * EACH, (parts[-1] + 1) * EACH)
        q = jnp.concatenate(
            [qx[tr, l, pl.ds(start + 8, HALF), :] for l, start in places for tr in tracers], axis=0
        )
        diff = q - cells
        part0 = diff.astype(jnp.bfloat16)
        rest = diff - part0.astype(jnp.float32)
        part1 = rest.astype(jnp.bfloat16)
        part2 = (rest - part1.astype(jnp.float32)).astype(jnp.bfloat16)
        sums = (
            jnp.dot(part2, upper, preferred_element_type=jnp.float32)
            + jnp.dot(part1, upper, preferred_element_type=jnp.float32)
        ) + jnp.dot(part0, upper, preferred_element_type=jnp.float32)
        frac = [cv[l, pl.ds(start, HALF), :] for l, start in places]
        west = [take(west_row, HALF * h + row8) for h in homes]
        weights = []
        for c in (frac, west):
            t = [1.0 - x for x in c]
            tt = [(x * x - x) * 0.25 for x in t]
            for w in (t, tt):
                weights.append(jnp.concatenate([x for x in w for _ in tracers], axis=0))
        t, tt, t_west, tt_west = weights
        offset = jnp.broadcast_to(ext_b[:, 0:1], (rows, LON))
        flux = sums - offset - (plus1 * t + (plus2 - cells) * tt)
        first_west = -ext_b - (cells * t_west + (plus1 - ext_a) * tt_west)
        flux_west = jnp.where(lane == 0, first_west, pltpu.roll(flux, 1, 1))
        change = flux - flux_west
        at = 0
        for l, start in places:
            for tr in tracers:
                spot = (tr, l, pl.ds(start, HALF), slice(None))
                flux_v[spot] = flux[at : at + HALF]
                base[spot] = base[spot] - change[at : at + HALF]
                at += HALF

    for first_part in range(0, PARTS, FIN):
        def step(d, carry):
            finish(range(first_part, first_part + FIN), d)
            return carry

        lax.fori_loop(1, 5, step, 0)
        if first_part == 0:
            for part in range(PARTS - 1):
                take_bytes(back.at[part, pl.ds(0, RING - 1), pl.ds(0, SIZE)], s2.at[part])
            for tr in range(TR):
                take_bytes(gat.at[tr, pl.ds(0, RING - 1)], s1.at[tr])
            for copy in halo:
                copy.wait_send()
            edge.wait_send()

    take_bytes(back.at[PARTS - 1, pl.ds(0, RING - 1), pl.ds(0, SIZE)], s2.at[PARTS - 1])


def hand_on(upd_in, flux_in, upd_out, flux_out, gone):
    legs = [
        pltpu.make_async_copy(src, dst, gone.at[i])
        for i, (src, dst) in enumerate(((upd_in, upd_out), (flux_in, flux_out)))
    ]
    for leg in legs:
        leg.start()
    for leg in legs:
        leg.wait()


def per_device(tracers, courant_frac, shifts, merid):
    vmem, dma, f32 = pltpu.VMEM, pltpu.SemaphoreType.DMA, jnp.float32
    shape = jax.ShapeDtypeStruct((TR, LEV, ROWS, LON), f32)
    anywhere = pl.BlockSpec(memory_space=pl.ANY)
    tall = -(-SIZE // 8) * 8
    held = pltpu.VMEM((TR, LEV, ROWS, LON), f32)
    inside = pl.BlockSpec(memory_space=pltpu.VMEM)
    inputs = [pltpu.with_memory_space_constraint(x, pltpu.HBM) for x in (tracers, courant_frac, shifts, merid)]
    updated, flux = pl.pallas_call(
        kernel,
        out_shape=(held, held),
        in_specs=[pl.BlockSpec(memory_space=pltpu.HBM)] * 4,
        out_specs=(inside, inside),
        scratch_shapes=[
            vmem((LEV, ROWS), jnp.int32),
            vmem((TR, LEV, 32, LON), f32),
            vmem((LEV, 32, LON), f32),
            vmem((LEV, ROWS, LON), f32),
            vmem((TR, RING, HALF, LON), f32),
            vmem((PARTS, RING, tall, LON), f32),
            vmem((PARTS, RING, tall, LON), f32),
            vmem((RING, HALF, LON), f32),
            vmem((HALF, LON), f32),
            vmem((HALF, LON), f32),
            dma((TR,)), dma((TR,)), dma((PARTS,)), dma((PARTS, 4)),
            dma((4,)), dma((3,)), dma((3,)), dma((1,)), dma((1,)),
            pltpu.SemaphoreType.REGULAR,
        ],
        compiler_params=pltpu.CompilerParams(collective_id=0, has_side_effects=True, vmem_limit_bytes=16 * 2**20),
        cost_estimate=pl.CostEstimate(flops=100_000_000, bytes_accessed=1_000_000, transcendentals=0),
    )(*inputs)
    return pl.pallas_call(
        hand_on,
        out_shape=(shape, shape),
        in_specs=[inside] * 2,
        out_specs=(anywhere, anywhere),
        scratch_shapes=[dma((2,))],
        compiler_params=pltpu.CompilerParams(vmem_limit_bytes=2**20),
        cost_estimate=pl.CostEstimate(flops=0, bytes_accessed=1_000_000, transcendentals=0),
    )(*(pltpu.with_memory_space_constraint(x, pltpu.VMEM) for x in (updated, flux)))


def solution(mesh):
    return jax.shard_map(
        per_device,
        mesh=mesh,
        in_specs=(
            P(None, None, "lat", "lon"),
            P(None, "lat", "lon"),
            P(None, "lat"),
            P(None, "lat", "lon"),
        ),
        out_specs=(P(None, None, "lat", "lon"), P(None, None, "lat", "lon")),
        check_vma=False,
    )
```

```python
import functools

import jax
import jax.numpy as jnp
from jax import lax
from jax.experimental import pallas as pl
from jax.experimental.pallas import tpu as pltpu
from jax.sharding import PartitionSpec as P

TR, LEV, ROWS, LON, RING, BANDS = 4, 8, 16, 128, 16, 16
NLAT = ROWS * BANDS
HALF = 8
REACH = 3
PARTS = 1
EACH = TR // PARTS
WIDE = EACH * HALF
SIZE = WIDE + 1
FIN = 1
MESH = pl.DeviceIdType.MESH
FAR = tuple(sorted(range(1, RING), key=lambda d: (-min(d % 8, 8 - d % 8), d)))
ORDER = (0, 8, 9, 1, 2, 10, 3, 11, 7, 15, 6, 14, 4, 12, 5, 13)


def lanes_iota(rows):
    return lax.broadcasted_iota(jnp.int32, (rows, LON), 1)


def rows_iota(rows):
    return lax.broadcasted_iota(jnp.int32, (rows, LON), 0)


def take(values, index):
    return jnp.take_along_axis(values, index, axis=1, mode="promise_in_bounds")


def ring(index):
    return jnp.bitwise_and(index, RING - 1)


def kernel(
    q_hbm, c_hbm, s_hbm, v_hbm, base, flux_v,
    s_ref, qx, mx, cv, gat, ret, back, pack, cw_out, cw_in,
    s1, r1, s2, r2, sl, sh, rh, se, re, ready,
):
    me = lax.axis_index("lon")
    lat = lax.axis_index("lat")

    own_q = pltpu.make_async_copy(q_hbm, qx.at[:, :, pl.ds(8, ROWS), :], sl.at[0])
    own_c = pltpu.make_async_copy(c_hbm, cv, sl.at[2])
    own_v = pltpu.make_async_copy(v_hbm, mx.at[:, pl.ds(8, ROWS), :], sl.at[3])
    own_s = pltpu.make_async_copy(s_hbm, s_ref, sl.at[1])
    own_q.start()

    barrier = pltpu.get_barrier_semaphore()
    north, south = ring(lat + 1), ring(lat + BANDS - 1)
    for d in FAR:
        pl.semaphore_signal(barrier, inc=1, device_id={"lon": ring(me + d)}, device_id_type=MESH)
    pl.semaphore_signal(barrier, inc=1, device_id={"lat": south}, device_id_type=MESH)

    def of_home(h, tr):
        return qx.at[tr, h // 2, pl.ds(pl.multiple_of(HALF + (h % 2) * HALF, HALF), HALF), :]

    for copy in (own_s, own_c, own_v):
        copy.start()

    lane8, row8 = lanes_iota(HALF), rows_iota(HALF)
    own_q.wait()
    pl.semaphore_wait(barrier, RING)

    def gather_copy(d, tr):
        target = ring(me + d)
        return pltpu.make_async_remote_copy(
            of_home(target, tr), gat.at[tr, me], s1.at[tr], r1.at[tr],
            device_id={"lon": target}, device_id_type=MESH,
        )

    for tr in range(TR):
        for d in FAR:
            gather_copy(d, tr).start()

    for tr in range(TR):
        pltpu.make_async_copy(of_home(me, tr), gat.at[tr, me], r1.at[tr]).start()

    halo = [
        (qx.at[:, :, pl.ds(8 + ROWS - 2, 2), :], qx.at[:, :, pl.ds(6, 2), :], north),
        (qx.at[:, :, pl.ds(8, 2), :], qx.at[:, :, pl.ds(24, 2), :], south),
        (v_hbm.at[:, pl.ds(ROWS - 1, 1), :], mx.at[:, pl.ds(7, 1), :], north),
    ]
    halo = [
        pltpu.make_async_remote_copy(a, b, sh.at[i], rh.at[i], device_id={"lat": p}, device_id_type=MESH)
        for i, (a, b, p) in enumerate(halo)
    ]
    pl.semaphore_signal(ready, inc=1, device_id={"lat": north}, device_id_type=MESH)
    halo[0].start()
    halo[2].start()
    own_c.wait()
    packed = jnp.zeros((HALF, LON), jnp.float32)
    for tile in range(2 * LEV):
        column = cv[tile // 2, HALF * (tile % 2) : HALF * (tile % 2) + HALF, LON - 1 : LON]
        packed = jnp.where(lane8 == HALF * tile + row8, column, packed)
    cw_out[...] = jnp.broadcast_to(jnp.sum(packed, axis=0, keepdims=True), (HALF, LON))
    edge = pltpu.make_async_remote_copy(
        cw_out, cw_in, se.at[0], re.at[0], device_id={"lon": ring(me + 1)}, device_id_type=MESH
    )
    edge.start()

    own_s.wait()
    line = s_ref[pl.ds(me // 2, 1), :].astype(jnp.float32)
    pick = lax.broadcasted_iota(jnp.int32, (HALF, ROWS), 1) == (
        lax.broadcasted_iota(jnp.int32, (HALF, ROWS), 0) + HALF * (me % 2)
    )
    shift = jnp.sum(jnp.where(pick, jnp.broadcast_to(line, (HALF, ROWS)), 0.0), axis=1, keepdims=True)
    first = -1 - jnp.broadcast_to(shift, (HALF, LON)).astype(jnp.int32)
    raised = first + REACH * LON
    low = jnp.right_shift(raised, 7)
    remain = jnp.bitwise_and(raised, LON - 1)
    hop = jnp.where(lane8 >= remain, low, low + 1)
    bits = [jnp.bitwise_and(hop, 1 << n) != 0 for n in range(3)]
    turn = jnp.bitwise_and(lane8 + remain, LON - 1)
    signs = []
    for off in range(-REACH, REACH):
        cell = off * LON + lane8
        if off < 0:
            signs.append(jnp.where(cell >= first, -1.0, 0.0))
        else:
            signs.append(jnp.where(cell < first, 1.0, 0.0))
    group = lane8 // WIDE
    ends = jnp.where(group == 0, LON - 1, jnp.where(group == 1, 0, 1))

    pl.semaphore_wait(ready, 1)
    halo[1].start()

    def away(t):
        hops = jnp.bitwise_and(t - me + RING, 7)
        hops = jnp.minimum(hops, 8 - hops)
        return jnp.where(hops == 0, 3, hops - 1)

    def return_copy(t, part, rows):
        return pltpu.make_async_remote_copy(
            ret.at[part, t, rows], back.at[part, me, rows], s2.at[part], r2.at[part, away(t)],
            device_id={"lon": t}, device_id_type=MESH,
        )

    def send_back(part, rows):
        for t in ORDER:
            @pl.when(t != me)
            def _():
                return_copy(t, part, rows).start()

        pltpu.make_async_copy(ret.at[part, me, rows], back.at[part, me, rows], r2.at[part, away(me)]).start()

    def take_bytes(ref, sem):
        pltpu.make_async_copy(ref, ref, sem).wait()

    for part in range(PARTS):
        for i in range(EACH):
            tr = part * EACH + i
            take_bytes(gat.at[tr], r1.at[tr])
            blocks = [gat[tr, b] for b in range(RING)]
            mine = ((lane8 // HALF) % EACH == i) & (lane8 % HALF == row8)
            one = [jnp.where(bits[0], blocks[(b - 2) % RING], blocks[(b - 3) % RING]) for b in range(RING)]
            two = [jnp.where(bits[1], one[(b + 2) % RING], one[b]) for b in range(RING)]
            aligned = [take(jnp.where(bits[2], two[(b + 4) % RING], two[b]), turn) for b in range(RING)]
            for b in range(RING):
                ret[part, b, HALF * i : HALF * i + HALF, :] = aligned[b]
            if i < EACH - 1:
                send_back(part, pl.ds(HALF * i, HALF))
            tips = [take(a, ends) for a in aligned]
            for b in range(RING):
                total = blocks[(b - REACH) % RING] * signs[0]
                for n in range(1, 2 * REACH):
                    total = total + blocks[(b - REACH + n) % RING] * signs[n]
                offset = jnp.sum(total, axis=1, keepdims=True)
                extra = jnp.where(group == 0, tips[b - 1], jnp.where(group == 3, offset, tips[(b + 1) % RING]))
                if i == 0:
                    pack[b] = jnp.where(mine, extra, 0.0)
                else:
                    pack[b] = jnp.where(mine, extra, pack[b])
        for b in range(RING):
            ret[part, b, WIDE:SIZE, :] = jnp.sum(pack[b], axis=0, keepdims=True)

        send_back(part, pl.ds(WIDE - HALF, HALF + 1))

    own_v.wait()
    for copy in halo:
        copy.wait_recv()
    face = lat * ROWS + rows_iota(ROWS)

    def meridional(l, carry):
        for o in (-1, 0):
            v = mx[l, 8 + o : 24 + o]
            v = jnp.where((face + o == NLAT - 1) | (face + o < 0), 0.0, v)
            up = v >= 0.0
            half_low = v * (1.0 - v) * 0.5
            half_high = v * (1.0 + v) * 0.5
            zero_low = (face + o <= 0) | (face + o >= NLAT - 1)
            zero_high = (face + o + 1 <= 0) | (face + o + 1 >= NLAT - 1)
            for tr in range(TR):
                q_low = qx[tr, l, 8 + o : 24 + o]
                q_high = qx[tr, l, 9 + o : 25 + o]
                side_low = jnp.where(zero_low, 0.0, 0.5 * (q_high - qx[tr, l, 7 + o : 23 + o]))
                side_high = jnp.where(zero_high, 0.0, 0.5 * (qx[tr, l, 10 + o : 26 + o] - q_low))
                flux = jnp.where(up, v * q_low + half_low * side_low, v * q_high - half_high * side_high)
                if o < 0:
                    base[tr, l] = qx[tr, l, 8:24] + flux
                else:
                    base[tr, l] = base[tr, l] - flux
        return carry

    lax.fori_loop(0, LEV, meridional, 0)

    edge.wait_recv()
    west_row = jnp.broadcast_to(cw_in[0:1, :], (HALF, LON))
    upper = jnp.where(
        lax.broadcasted_iota(jnp.int32, (LON, LON), 0) <= lax.broadcasted_iota(jnp.int32, (LON, LON), 1), 1.0, 0.0
    ).astype(jnp.bfloat16)
    rows = 4 * FIN * WIDE
    lane, row = lanes_iota(rows), rows_iota(rows) % WIDE
    index_a = jnp.where(lane == LON - 2, 1, jnp.where(lane == LON - 1, 2, 0)) * WIDE + row
    index_b = jnp.where(lane == LON - 1, 1, 3) * WIDE + row

    def finish(parts, d):
        past = jnp.where(d == 4, 4, 0)
        homes = [ring(me + d), ring(me + RING - d), ring(me + 8 + d + past), ring(me + 8 - d + past)]
        places = [(h // 2, pl.multiple_of((h % 2) * HALF, HALF)) for h in homes]
        for part in parts:
            take_bytes(back.at[part, pl.ds(0, 4), pl.ds(0, SIZE)], r2.at[part, d - 1])
        cells = jnp.concatenate([back[part, h, 0:WIDE] for h in homes for part in parts], axis=0)
        extra = jnp.concatenate(
            [jnp.broadcast_to(back[part, h, WIDE:SIZE], (WIDE, LON)) for h in homes for part in parts], axis=0
        )
        ext_a, ext_b = take(extra, index_a), take(extra, index_b)
        plus1 = jnp.where(lane == LON - 1, ext_b, pltpu.roll(cells, LON - 1, 1))
        plus2 = jnp.where(lane >= LON - 2, ext_a, pltpu.roll(cells, LON - 2, 1))
        tracers = range(parts[0] * EACH, (parts[-1] + 1) * EACH)
        q = jnp.concatenate(
            [qx[tr, l, pl.ds(start + 8, HALF), :] for l, start in places for tr in tracers], axis=0
        )
        diff = q - cells
        part0 = diff.astype(jnp.bfloat16)
        rest = diff - part0.astype(jnp.float32)
        part1 = rest.astype(jnp.bfloat16)
        part2 = (rest - part1.astype(jnp.float32)).astype(jnp.bfloat16)
        sums = (
            jnp.dot(part2, upper, preferred_element_type=jnp.float32)
            + jnp.dot(part1, upper, preferred_element_type=jnp.float32)
        ) + jnp.dot(part0, upper, preferred_element_type=jnp.float32)
        frac = [cv[l, pl.ds(start, HALF), :] for l, start in places]
        west = [take(west_row, HALF * h + row8) for h in homes]
        weights = []
        for c in (frac, west):
            t = [1.0 - x for x in c]
            tt = [(x * x - x) * 0.25 for x in t]
            for w in (t, tt):
                weights.append(jnp.concatenate([x for x in w for _ in tracers], axis=0))
        t, tt, t_west, tt_west = weights
        offset = jnp.broadcast_to(ext_b[:, 0:1], (rows, LON))
        flux = sums - offset - (plus1 * t + (plus2 - cells) * tt)
        first_west = -ext_b - (cells * t_west + (plus1 - ext_a) * tt_west)
        flux_west = jnp.where(lane == 0, first_west, pltpu.roll(flux, 1, 1))
        change = flux - flux_west
        at = 0
        for l, start in places:
            for tr in tracers:
                spot = (tr, l, pl.ds(start, HALF), slice(None))
                flux_v[spot] = flux[at : at + HALF]
                base[spot] = base[spot] - change[at : at + HALF]
                at += HALF

    for first_part in range(0, PARTS, FIN):
        def step(d, carry):
            finish(range(first_part, first_part + FIN), d)
            return carry

        lax.fori_loop(1, 5, step, 0)
        if first_part == 0:
            for part in range(PARTS - 1):
                take_bytes(back.at[part, pl.ds(0, RING - 1), pl.ds(0, SIZE)], s2.at[part])
            for tr in range(TR):
                take_bytes(gat.at[tr, pl.ds(0, RING - 1)], s1.at[tr])
            for copy in halo:
                copy.wait_send()
            edge.wait_send()

    take_bytes(back.at[PARTS - 1, pl.ds(0, RING - 1), pl.ds(0, SIZE)], s2.at[PARTS - 1])


def hand_on(upd_in, flux_in, upd_out, flux_out, gone):
    legs = [
        pltpu.make_async_copy(src, dst, gone.at[i])
        for i, (src, dst) in enumerate(((upd_in, upd_out), (flux_in, flux_out)))
    ]
    for leg in legs:
        leg.start()
    for leg in legs:
        leg.wait()


def per_device(tracers, courant_frac, shifts, merid):
    vmem, dma, f32 = pltpu.VMEM, pltpu.SemaphoreType.DMA, jnp.float32
    shape = jax.ShapeDtypeStruct((TR, LEV, ROWS, LON), f32)
    anywhere = pl.BlockSpec(memory_space=pl.ANY)
    tall = -(-SIZE // 8) * 8
    held = pltpu.VMEM((TR, LEV, ROWS, LON), f32)
    inside = pl.BlockSpec(memory_space=pltpu.VMEM)
    inputs = [pltpu.with_memory_space_constraint(x, pltpu.HBM) for x in (tracers, courant_frac, shifts, merid)]
    updated, flux = pl.pallas_call(
        kernel,
        out_shape=(held, held),
        in_specs=[pl.BlockSpec(memory_space=pltpu.HBM)] * 4,
        out_specs=(inside, inside),
        scratch_shapes=[
            vmem((LEV, ROWS), jnp.int32),
            vmem((TR, LEV, 32, LON), f32),
            vmem((LEV, 32, LON), f32),
            vmem((LEV, ROWS, LON), f32),
            vmem((TR, RING, HALF, LON), f32),
            vmem((PARTS, RING, tall, LON), f32),
            vmem((PARTS, RING, tall, LON), f32),
            vmem((RING, HALF, LON), f32),
            vmem((HALF, LON), f32),
            vmem((HALF, LON), f32),
            dma((TR,)), dma((TR,)), dma((PARTS,)), dma((PARTS, 4)),
            dma((4,)), dma((3,)), dma((3,)), dma((1,)), dma((1,)),
            pltpu.SemaphoreType.REGULAR,
        ],
        compiler_params=pltpu.CompilerParams(collective_id=0, has_side_effects=True, vmem_limit_bytes=16 * 2**20),
        cost_estimate=pl.CostEstimate(flops=100_000_000, bytes_accessed=1_000_000, transcendentals=0),
    )(*inputs)
    return pl.pallas_call(
        hand_on,
        out_shape=(shape, shape),
        in_specs=[inside] * 2,
        out_specs=(anywhere, anywhere),
        scratch_shapes=[dma((2,))],
        compiler_params=pltpu.CompilerParams(vmem_limit_bytes=2**20),
        cost_estimate=pl.CostEstimate(flops=0, bytes_accessed=1_000_000, transcendentals=0),
    )(*(pltpu.with_memory_space_constraint(x, pltpu.VMEM) for x in (updated, flux)))


def solution(mesh):
    return jax.shard_map(
        per_device,
        mesh=mesh,
        in_specs=(
            P(None, None, "lat", "lon"),
            P(None, "lat", "lon"),
            P(None, "lat"),
            P(None, "lat", "lon"),
        ),
        out_specs=(P(None, None, "lat", "lon"), P(None, None, "lat", "lon")),
        check_vma=False,
    )
```
